512 devices in a mesh: cuts: 32 (over z, x_lo), blk: 16 (over x_hi, y, core).
Axes of the slice: x: 4 (x_hi: 2, x_lo: 2; x = x_hi * 2 + x_lo), y: 4, z: 16, core: 2. Of those that a mesh axis runs over, the one named last changes fastest.
Arguments:
- steps: bfloat16 [512, 2, 512, 512], P(('cuts', 'blk')), as said below
Outputs:
- sidebands: float32 [32, 2, 512, 512], P(None, None, 'blk', 'cuts')
Inputs may be any that keep to these rules, and one draw needn't show every extreme that they name: `steps`: sqrt(512) times every entry lies between -1 and 1.
All inputs are finite; a program needn't handle non-finite values.
Results may differ from the reference program's by a relative error of at most 0.035.
Values may be sent and summed in bfloat16 or wider, within the bound.
A program may use at most 64 MiB of HBM per device.

```python
import math
import jax
import jax.numpy as jnp
from jax import lax

M = 512
STEPS = 512
N_CUTS = 32
N_BLK = 16


def draw_steps(key, part):
    key_row, key_col, key_jitter = jax.random.split(key, 3)
    positions = jnp.arange(M, dtype=jnp.int32)
    fourier_phase = (positions[:, None] * positions[None, :] % M).astype(jnp.float32) * (2.0 * math.pi / M)
    row_phase = jax.random.uniform(key_row, (STEPS, M, 1), jnp.float32, 0.0, 2.0 * math.pi)
    col_phase = jax.random.uniform(key_col, (STEPS, 1, M), jnp.float32, 0.0, 2.0 * math.pi)
    jitter = 0.02 * jax.random.normal(key_jitter, (STEPS, M, M), jnp.float32)
    total_phase = fourier_phase[None] + row_phase + col_phase + jitter
    norm_factor = 1.0 / math.sqrt(M)
    result = jnp.stack([jnp.cos(total_phase), jnp.sin(total_phase)], axis=1) * norm_factor
    return result.astype(jnp.bfloat16)


def setup_inputs(seed: int = 0) -> dict:
    streams_of = jax.random.split(jax.random.key(seed), 2)
    return {
        "steps": draw_steps(jax.random.fold_in(streams_of[1], 71), 0),
    }


def complex_product(left_factor, right_factor):
    left_real = left_factor[0].astype(jnp.float32)
    left_imag = left_factor[1].astype(jnp.float32)
    right_real = right_factor[0].astype(jnp.float32)
    right_imag = right_factor[1].astype(jnp.float32)
    hp = lax.Precision.HIGHEST
    real_part = jnp.dot(left_real, right_real, precision=hp) - jnp.dot(left_imag, right_imag, precision=hp)
    imag_part = jnp.dot(left_real, right_imag, precision=hp) + jnp.dot(left_imag, right_real, precision=hp)
    return jnp.stack([real_part, imag_part])

def pair_product(factor_pair):
    return complex_product(factor_pair[0], factor_pair[1]).astype(jnp.bfloat16)

def wide_product(factor_pair):
    return complex_product(factor_pair[0], factor_pair[1])

def slice_product(factors):
    while factors.shape[0] > 1:
        factors = lax.map(wide_product, (factors[1::2], factors[0::2]))
    return factors[0].astype(jnp.bfloat16)

def reference(steps):
    step_grid = steps.reshape(N_CUTS, N_BLK, 2, M, M)
    products = lax.map(slice_product, step_grid)
    distance = 1
    while distance < N_CUTS:
        ahead = jnp.roll(products, -distance, axis=0)
        products = lax.map(pair_product, (ahead, products))
        distance = distance * 2
    freq_index = jnp.arange(N_CUTS, dtype=jnp.int32)
    phase_angle = 2.0 * math.pi / N_CUTS * (freq_index[:, None] * freq_index[None, :] % N_CUTS).astype(jnp.float32)
    cosine_table = jnp.cos(phase_angle)
    sine_table = jnp.sin(phase_angle)
    flattened = products.astype(jnp.float32).reshape(N_CUTS, 2, M * M)
    hp = lax.Precision.HIGHEST
    real_part = jnp.dot(cosine_table, flattened[:, 0], precision=hp) + jnp.dot(sine_table, flattened[:, 1], precision=hp)
    imag_part = jnp.dot(cosine_table, flattened[:, 1], precision=hp) - jnp.dot(sine_table, flattened[:, 0], precision=hp)
    norm_factor = math.sqrt(M / N_CUTS)
    result = jnp.stack([real_part, imag_part], axis=1) * norm_factor
    return result.reshape(N_CUTS, 2, M, M)
```

```python
import math

import jax
import jax.numpy as jnp
from jax import lax
from jax.experimental import pallas as pl
from jax.experimental.pallas import tpu as pltpu
from jax.sharding import PartitionSpec as P

MESH = pl.DeviceIdType.MESH
F32 = jnp.float32
BF16 = jnp.bfloat16
LEVELS = 5


def dot(a, b):
    return jnp.dot(a, b, preferred_element_type=F32)


def arrived(ref, sem):
    pltpu.make_async_copy(ref, ref, sem).wait()


def send(src, dst, send_sem, recv_sem, device):
    pltpu.make_async_remote_copy(
        src_ref=src,
        dst_ref=dst,
        send_sem=send_sem,
        recv_sem=recv_sem,
        device_id=device,
        device_id_type=MESH,
    ).start()


def combine(by_real, by_imag):
    rows = by_real.shape[0] // 2
    return by_real[:rows] - by_imag[rows:], by_imag[:rows] + by_real[rows:]


def halves(value):
    high = value.astype(BF16)
    return high, (value - high.astype(F32)).astype(BF16)


def kernel(
    x_ref, o_ref,
    left, right, pairs, pair_low, chain, acc, ends, sibling, shifted, gathered, period, tiles, landed,
    left_sem, right_sem, left_out, right_out, pair_sem, pair_out, chain_sem, chain_out,
    ends_sem, ends_out, sib_sem, sib_out, shift_sem, shift_out, gather_sem, gather_out, all_sem, all_out,
):
    c = lax.axis_index("cuts")
    b = lax.axis_index("blk")
    xh = lax.div(b, 8)
    y = lax.rem(lax.div(b, 2), 4)
    h = lax.rem(b, 2)
    other = 1 - h
    sib = (c, b + 1 - 2 * h)
    opposite = (c, b + 8 - 16 * xh)

    def along_y(d):
        return (c, xh * 8 + lax.rem(y + d, 4) * 2 + h)

    def cut(k):
        return (lax.rem(c + k + 32, 32), b)

    @pl.when(h == 0)
    def _():
        pltpu.make_async_copy(x_ref.at[0, :, :, pl.ds(0, 256)], right, right_sem).start()

    @pl.when(h == 1)
    def _():
        for r in range(4):
            for q in range(2):
                pltpu.make_async_copy(
                    x_ref.at[0, :, pl.ds(128 * r, 128), pl.ds(256 * q, 256)],
                    left.at[q, :, pl.ds(128 * r, 128)],
                    left_sem.at[r, q],
                ).start()

    barrier = pltpu.get_barrier_semaphore()
    greet = [sib, opposite] + [along_y(d) for d in (1, 2, 3)] + [cut(1 << s) for s in range(LEVELS)]
    for device in greet:
        pl.semaphore_signal(barrier, inc=1, device_id=device, device_id_type=MESH)
    pl.semaphore_wait(barrier, len(greet))

    @pl.when(h == 0)
    def _():
        send(x_ref.at[0, :, :, pl.ds(256, 256)], right, right_out, right_sem, sib)

    @pl.when(h == 1)
    def _():
        for r in range(4):
            for q in range(2):
                send(
                    x_ref.at[0, :, pl.ds(128 * r, 128), pl.ds(256 * q, 256)],
                    left.at[q, :, pl.ds(128 * r, 128)],
                    left_out.at[r, q],
                    left_sem.at[r, q],
                    sib,
                )

    arrived(right, right_sem)

    def pair_chunk(r, carry):
        rows = pl.ds(pl.multiple_of(128 * r, 128), 128)
        for q in range(2):
            arrived(left.at[q, :, rows], left_sem.at[r, q])
        x0 = left[0, :, rows, :].reshape(256, 256)
        x1 = left[1, :, rows, :].reshape(256, 256)
        by = [dot(x0, right[i, :256]) + dot(x1, right[i, 256:]) for i in range(2)]
        for i, part in enumerate(combine(*by)):
            high, low = halves(part)
            pairs[y, i, rows, :] = high
            pair_low[i, rows, :] = low
        for d in (1, 3, 2):
            block = pairs.at[y, :, rows]
            send(block, block, pair_out.at[d - 1, r], pair_sem.at[d - 1, r], along_y(d))
        return carry

    lax.fori_loop(0, 4, pair_chunk, 0)

    def wait_pair(j):
        @pl.when(y != j)
        def _():
            d = lax.rem(y - j + 4, 4)
            for r in range(4):
                arrived(pairs.at[j, :, pl.ds(128 * r, 128)], pair_sem.at[d - 1, r])

    def exchange_chain(s):
        send(chain.at[s, h], chain.at[s, h], chain_out.at[s], chain_sem.at[s], sib)

    wait_pair(3)
    for i in range(2):
        for p in range(2):
            rows = pl.ds(pl.multiple_of(256 * p + 64 * y, 64), 64)
            chain[0, h, 0, i, p] = pairs[3, i, rows, :]
            low = pair_low[i, rows, :]
            chain[0, h, 1, i, p] = jnp.where(y == 3, low, jnp.zeros_like(low))
    exchange_chain(0)
    for s in range(3):
        j = 2 - s
        wait_pair(j)
        arrived(chain.at[s, other], chain_sem.at[s])
        x0 = chain[s, 0].reshape(512, 256)
        x1 = chain[s, 1].reshape(512, 256)
        for i in range(2):
            t = dot(x0, pairs[j, i, :256]) + dot(x1, pairs[j, i, 256:])
            acc[i] = t[:256] + t[256:]

        @pl.when(y == j)
        def _():
            for i in range(2):
                acc[i] += dot(x0[:256], pair_low[i, :256]) + dot(x1[:256], pair_low[i, 256:])

        for i, part in enumerate(combine(acc[0], acc[1])):
            part = part.reshape(2, 64, 256)
            if s < 2:
                chain[s + 1, h, 0, i], chain[s + 1, h, 1, i] = halves(part)
            else:
                ends[xh, i] = part.astype(BF16)
        if s < 2:
            exchange_chain(s + 1)

    def spread(src, level):
        for d in (1, 3, 2):
            send(
                src, gathered.at[level, :, :, y],
                gather_out.at[level, d - 1], gather_sem.at[level, d - 1], along_y(d),
            )

    def product(own, level):
        for d in (1, 2, 3):
            arrived(gathered.at[level, :, :, lax.rem(y - d + 4, 4)], gather_sem.at[level, d - 1])
        x0 = own[...].reshape(256, 256)
        by = [dot(x0, gathered[level, i, h].reshape(256, 256)) for i in range(2)]
        arrived(sibling.at[level], sib_sem.at[level])
        x1 = sibling[level].reshape(256, 256)
        by = [by[i] + dot(x1, gathered[level, i, other].reshape(256, 256)) for i in range(2)]
        for i, part in enumerate(combine(*by)):
            part = part.reshape(2, 64, 256).astype(BF16)
            period[level, i] = part
            gathered[level + 1, i, :, y] = part

    send(ends.at[xh], ends.at[xh], ends_out, ends_sem, opposite)
    arrived(ends.at[1 - xh], ends_sem)
    spread(ends.at[0], 0)
    send(ends.at[1], sibling.at[0], sib_out.at[0], sib_sem.at[0], sib)
    gathered[0, :, :, y] = ends[0]
    product(ends.at[1], 0)

    def double(level, k):
        send(period.at[level], shifted.at[level], shift_out.at[level], shift_sem.at[level], cut(-k))
        spread(period.at[level], level + 1)
        arrived(shifted.at[level], shift_sem.at[level])
        send(shifted.at[level], sibling.at[level + 1], sib_out.at[level + 1], sib_sem.at[level + 1], sib)
        product(shifted.at[level], level + 1)
        return 2 * k

    lax.fori_loop(0, LEVELS, double, jnp.int32(1))

    final = period[LEVELS, :, xh].astype(F32)
    stacked = jnp.concatenate([final[0, :32], final[1, :32], final[0, 32:], final[1, 32:]], axis=0)
    turned = stacked.T
    tiles[0] = turned.astype(BF16).reshape(16, 16, 128)
    turned = jnp.concatenate([turned[:, 64:], turned[:, :64]], axis=1)
    tiles[1] = turned.astype(BF16).reshape(16, 16, 128)

    def scatter(j, carry):
        target = 16 * h + j
        for core in range(2):
            here = (target == c) & (h == core)

            @pl.when(here)
            def _():
                pltpu.make_async_copy(tiles.at[core, j], landed.at[c], all_sem).start()

            @pl.when(jnp.logical_not(here))
            def _():
                send(
                    tiles.at[core, j], landed.at[c], all_out.at[core, j], all_sem,
                    (target, xh * 8 + y * 2 + core),
                )
        return carry

    lax.fori_loop(0, 16, scatter, 0)

    @pl.when(h == 0)
    def _():
        arrived(right, right_out)

    @pl.when(h == 1)
    def _():
        for r in range(4):
            for q in range(2):
                arrived(left.at[q, :, pl.ds(128 * r, 128)], left_out.at[r, q])

    for d in range(3):
        for r in range(4):
            arrived(pairs.at[y, :, pl.ds(128 * r, 128)], pair_out.at[d, r])
    for s in range(3):
        arrived(chain.at[s, h], chain_out.at[s])
    arrived(ends.at[xh], ends_out)

    def level_sent(level, carry):
        for d in range(3):
            arrived(gathered.at[level, :, :, y], gather_out.at[level, d])
        arrived(sibling.at[level], sib_out.at[level])
        return carry

    lax.fori_loop(0, LEVELS + 1, level_sent, 0)

    def shift_sent(level, carry):
        arrived(period.at[level], shift_out.at[level])
        return carry

    lax.fori_loop(0, LEVELS, shift_sent, 0)

    def scatter_sent(j, carry):
        for core in range(2):
            @pl.when(jnp.logical_not((16 * h + j == c) & (h == core)))
            def _():
                arrived(tiles.at[core, j], all_out.at[core, j])
        return carry

    lax.fori_loop(0, 16, scatter_sent, 0)
    arrived(landed, all_sem)
    o_ref[...] = landed[...]


def per_device(steps):
    dma = pltpu.SemaphoreType.DMA
    landed = pl.pallas_call(
        kernel,
        out_shape=jax.ShapeDtypeStruct((32, 16, 128), BF16),
        in_specs=[pl.BlockSpec(memory_space=pl.ANY)],
        out_specs=pl.BlockSpec(memory_space=pltpu.VMEM),
        scratch_shapes=[
            pltpu.VMEM((2, 2, 512, 256), BF16),
            pltpu.VMEM((2, 512, 256), BF16),
            pltpu.VMEM((4, 2, 512, 256), BF16),
            pltpu.VMEM((2, 512, 256), BF16),
            pltpu.VMEM((3, 2, 2, 2, 2, 64, 256), BF16),
            pltpu.VMEM((2, 256, 256), F32),
            pltpu.VMEM((2, 2, 2, 64, 256), BF16),
            pltpu.VMEM((LEVELS + 1, 2, 2, 64, 256), BF16),
            pltpu.VMEM((LEVELS, 2, 2, 64, 256), BF16),
            pltpu.VMEM((LEVELS + 2, 2, 2, 4, 64, 256), BF16),
            pltpu.VMEM((LEVELS + 1, 2, 2, 64, 256), BF16),
            pltpu.VMEM((2, 16, 16, 128), BF16),
            pltpu.VMEM((32, 16, 128), BF16),
            dma((4, 2)), dma, dma((4, 2)), dma,
            dma((3, 4)), dma((3, 4)), dma((3,)), dma((3,)),
            dma, dma, dma((LEVELS + 1,)), dma((LEVELS + 1,)),
            dma((LEVELS,)), dma((LEVELS,)), dma((LEVELS + 1, 3)), dma((LEVELS + 1, 3)),
            dma, dma((2, 16)),
        ],
        compiler_params=pltpu.CompilerParams(
            collective_id=0, has_side_effects=True, vmem_limit_bytes=40 * 1024 * 1024
        ),
        cost_estimate=pl.CostEstimate(
            flops=8 * 512 * 512 * 512 * 3, bytes_accessed=4 * 1024 * 1024, transcendentals=0
        ),
        name="propagate",
    )(steps)
    count = 32
    index = jnp.arange(count, dtype=jnp.int32)
    angle = 2.0 * math.pi / count * (index[:, None] * index[None, :] % count).astype(F32)
    cosine, sine = jnp.cos(angle), jnp.sin(angle)
    values = landed.astype(F32)
    real_in = values[:, :, :32].reshape(count, 512)
    imag_in = values[:, :, 32:64].reshape(count, 512)
    hp = lax.Precision.HIGHEST
    real = jnp.dot(cosine, real_in, precision=hp) + jnp.dot(sine, imag_in, precision=hp)
    imag = jnp.dot(cosine, imag_in, precision=hp) - jnp.dot(sine, real_in, precision=hp)
    result = jnp.stack([real, imag], axis=1) * math.sqrt(512 / count)
    return result.reshape(count, 2, 16, 32).transpose(0, 1, 3, 2)


def solution(mesh):
    return jax.shard_map(
        per_device,
        mesh=mesh,
        in_specs=(P(("cuts", "blk"), None, None, None),),
        out_specs=P(None, None, "blk", "cuts"),
        check_vma=False,
    )
```

```python
import math

import jax
import jax.numpy as jnp
from jax import lax
from jax.experimental import pallas as pl
from jax.experimental.pallas import tpu as pltpu
from jax.sharding import PartitionSpec as P

MESH = pl.DeviceIdType.MESH
F32 = jnp.float32
BF16 = jnp.bfloat16
LEVELS = 5
WIDE = 3


def dot(a, b):
    return jnp.dot(a, b, preferred_element_type=F32)


def arrived(ref, sem):
    pltpu.make_async_copy(ref, ref, sem).wait()


def send(src, dst, send_sem, recv_sem, device):
    pltpu.make_async_remote_copy(
        src_ref=src,
        dst_ref=dst,
        send_sem=send_sem,
        recv_sem=recv_sem,
        device_id=device,
        device_id_type=MESH,
    ).start()


def combine(by_real, by_imag):
    rows = by_real.shape[0] // 2
    return by_real[:rows] - by_imag[rows:], by_imag[:rows] + by_real[rows:]


def halves(value):
    high = value.astype(BF16)
    return high, (value - high.astype(F32)).astype(BF16)


def kernel(
    x_ref, o_ref,
    left, right, pairs, pair_low, chain, acc, ends, sibling, shifted, gathered, period,
    late_shift, late_sib, late, tiles, landed,
    left_sem, right_sem, left_out, right_out, pair_sem, pair_out, chain_sem, chain_out,
    ends_sem, ends_out, sib_sem, sib_out, shift_sem, shift_out, gather_sem, gather_out,
    late_sem, late_out, all_sem, all_out,
):
    c = lax.axis_index("cuts")
    b = lax.axis_index("blk")
    xh = lax.div(b, 8)
    y = lax.rem(lax.div(b, 2), 4)
    h = lax.rem(b, 2)
    other = 1 - h
    sib = (c, b + 1 - 2 * h)
    opposite = (c, b + 8 - 16 * xh)

    def along_y(d):
        return (c, xh * 8 + lax.rem(y + d, 4) * 2 + h)

    def cut(k):
        return (lax.rem(c + k + 32, 32), b)

    @pl.when(h == 0)
    def _():
        pltpu.make_async_copy(x_ref.at[0, :, :, pl.ds(0, 256)], right, right_sem).start()

    @pl.when(h == 1)
    def _():
        for r in range(4):
            for q in range(2):
                pltpu.make_async_copy(
                    x_ref.at[0, :, pl.ds(128 * r, 128), pl.ds(256 * q, 256)],
                    left.at[q, :, pl.ds(128 * r, 128)],
                    left_sem.at[r, q],
                ).start()

    barrier = pltpu.get_barrier_semaphore()
    greet = [sib, opposite] + [along_y(d) for d in (1, 2, 3)] + [cut(1 << s) for s in range(LEVELS)]
    for device in greet:
        pl.semaphore_signal(barrier, inc=1, device_id=device, device_id_type=MESH)
    pl.semaphore_wait(barrier, len(greet))

    @pl.when(h == 0)
    def _():
        send(x_ref.at[0, :, :, pl.ds(256, 256)], right, right_out, right_sem, sib)

    @pl.when(h == 1)
    def _():
        for r in range(4):
            for q in range(2):
                send(
                    x_ref.at[0, :, pl.ds(128 * r, 128), pl.ds(256 * q, 256)],
                    left.at[q, :, pl.ds(128 * r, 128)],
                    left_out.at[r, q],
                    left_sem.at[r, q],
                    sib,
                )

    arrived(right, right_sem)

    def pair_chunk(r, carry):
        rows = pl.ds(pl.multiple_of(128 * r, 128), 128)
        for q in range(2):
            arrived(left.at[q, :, rows], left_sem.at[r, q])
        x0 = left[0, :, rows, :].reshape(256, 256)
        x1 = left[1, :, rows, :].reshape(256, 256)
        by = [dot(x0, right[i, :256]) + dot(x1, right[i, 256:]) for i in range(2)]
        for i, part in enumerate(combine(*by)):
            high, low = halves(part)
            pairs[y, i, rows, :] = high
            pair_low[i, rows, :] = low
        for d in (1, 3, 2):
            block = pairs.at[y, :, rows]
            send(block, block, pair_out.at[d - 1, r], pair_sem.at[d - 1, r], along_y(d))
        return carry

    lax.fori_loop(0, 4, pair_chunk, 0)

    def wait_pair(j):
        @pl.when(y != j)
        def _():
            d = lax.rem(y - j + 4, 4)
            for r in range(4):
                arrived(pairs.at[j, :, pl.ds(128 * r, 128)], pair_sem.at[d - 1, r])

    def exchange_chain(s):
        send(chain.at[s, h], chain.at[s, h], chain_out.at[s], chain_sem.at[s], sib)

    wait_pair(3)
    for i in range(2):
        for p in range(2):
            rows = pl.ds(pl.multiple_of(256 * p + 64 * y, 64), 64)
            chain[0, h, 0, i, p] = pairs[3, i, rows, :]
            low = pair_low[i, rows, :]
            chain[0, h, 1, i, p] = jnp.where(y == 3, low, jnp.zeros_like(low))
    exchange_chain(0)
    for s in range(3):
        j = 2 - s
        wait_pair(j)
        arrived(chain.at[s, other], chain_sem.at[s])
        x0 = chain[s, 0].reshape(512, 256)
        x1 = chain[s, 1].reshape(512, 256)
        for i in range(2):
            t = dot(x0, pairs[j, i, :256]) + dot(x1, pairs[j, i, 256:])
            acc[i] = t[:256] + t[256:]

        @pl.when(y == j)
        def _():
            for i in range(2):
                acc[i] += dot(x0[:256], pair_low[i, :256]) + dot(x1[:256], pair_low[i, 256:])

        for i, part in enumerate(combine(acc[0], acc[1])):
            part = part.reshape(2, 64, 256)
            if s < 2:
                chain[s + 1, h, 0, i], chain[s + 1, h, 1, i] = halves(part)
            else:
                ends[xh, i] = part.astype(BF16)
        if s < 2:
            exchange_chain(s + 1)

    def spread(src, level, order, p):
        for d in (1, 3, 2):
            send(
                src, gathered.at[level, :, p, y],
                gather_out.at[level, order, d - 1], gather_sem.at[level, order, d - 1], along_y(d),
            )

    def spread_arrived(level, order, p):
        for d in (1, 2, 3):
            arrived(gathered.at[level, :, p, lax.rem(y - d + 4, 4)], gather_sem.at[level, order, d - 1])

    def half_product(x, level, p):
        return [dot(x, gathered[level, i, p].reshape(256, 256)) for i in range(2)]

    def product(own, theirs, theirs_sem, level):
        rows = 2 * math.prod(own.shape[1:-1])
        spread_arrived(level, 0, h)
        by = half_product(own[...].reshape(rows, 256), level, h)
        arrived(theirs, theirs_sem)
        spread_arrived(level, 1, other)
        more = half_product(theirs[...].reshape(rows, 256), level, other)
        return combine(by[0] + more[0], by[1] + more[1])

    def keep(parts, level):
        for i, part in enumerate(parts):
            part = part.reshape(2, 64, 256).astype(BF16)
            period[level, i] = part
            gathered[level + 1, i, :, y] = part

    for order, p in enumerate((h, other)):
        send(ends.at[xh, :, p], ends.at[xh, :, p], ends_out.at[order], ends_sem.at[order], opposite)
    for order, p in enumerate((h, other)):
        arrived(ends.at[1 - xh, :, p], ends_sem.at[order])
        spread(ends.at[0, :, p], 0, order, p)
    send(ends.at[1], sibling.at[0], sib_out.at[0], sib_sem.at[0], sib)
    gathered[0, :, :, y] = ends[0]
    keep(product(ends.at[1], sibling.at[0], sib_sem.at[0], 0), 0)

    def double(level, k):
        send(period.at[level], shifted.at[level], shift_out.at[level], shift_sem.at[level], cut(-k))
        for order, p in enumerate((h, other)):
            spread(period.at[level, :, p], level + 1, order, p)
        arrived(shifted.at[level], shift_sem.at[level])
        after = level + 1
        send(shifted.at[level], sibling.at[after], sib_out.at[after], sib_sem.at[after], sib)
        keep(product(shifted.at[level], sibling.at[after], sib_sem.at[after], after), after)
        return 2 * k

    lax.fori_loop(0, WIDE, double, jnp.int32(1))

    send(period.at[WIDE, :, xh], late_shift.at[0], late_out.at[0], late_sem.at[0], cut(-8))
    for order, p in enumerate((h, other)):
        spread(period.at[WIDE, :, p], WIDE + 1, order, p)
    arrived(late_shift.at[0], late_sem.at[0])
    send(late_shift.at[0], late_sib.at[0], late_out.at[1], late_sem.at[1], sib)
    for i, part in enumerate(product(late_shift.at[0], late_sib.at[0], late_sem.at[1], WIDE + 1)):
        part = part.astype(BF16)
        late[0, i] = part
        gathered[WIDE + 2, i, xh, y] = part

    send(late.at[0], late_shift.at[1], late_out.at[2], late_sem.at[2], cut(-16))
    send(late.at[0], late.at[1], late_out.at[3], late_sem.at[3], opposite)
    level = WIDE + 2
    spread(late.at[0], level, lax.rem(xh + h, 2), xh)
    arrived(late.at[1], late_sem.at[3])
    spread(late.at[1], level, lax.rem(1 - xh + h, 2), 1 - xh)
    gathered[level, :, 1 - xh, y] = late[1]
    arrived(late_shift.at[1], late_sem.at[2])
    send(late_shift.at[1], late_sib.at[1], late_out.at[4], late_sem.at[4], sib)
    real, imag = product(late_shift.at[1], late_sib.at[1], late_sem.at[4], level)

    stacked = jnp.concatenate([real[:32], imag[:32], real[32:], imag[32:]], axis=0)
    turned = stacked.T
    tiles[0] = turned.astype(BF16).reshape(16, 16, 128)
    turned = jnp.concatenate([turned[:, 64:], turned[:, :64]], axis=1)
    tiles[1] = turned.astype(BF16).reshape(16, 16, 128)
    same = lax.div(c, 16) == h

    def nearness(t):
        t = jnp.where(same, 15 - t, t)
        step = lax.div(t + 1, 2)
        return lax.rem(c + jnp.where(lax.rem(t, 2) == 1, step, 16 - step), 16)

    def scatter(t, carry):
        j = nearness(t)
        target = 16 * h + j
        for core in range(2):
            here = (target == c) & (h == core)

            @pl.when(here)
            def _():
                pltpu.make_async_copy(tiles.at[core, j], landed.at[c], all_sem).start()

            @pl.when(jnp.logical_not(here))
            def _():
                send(
                    tiles.at[core, j], landed.at[c], all_out.at[core, j], all_sem,
                    (target, xh * 8 + y * 2 + core),
                )
        return carry

    lax.fori_loop(0, 16, scatter, 0)

    @pl.when(h == 0)
    def _():
        arrived(right, right_out)

    @pl.when(h == 1)
    def _():
        for r in range(4):
            for q in range(2):
                arrived(left.at[q, :, pl.ds(128 * r, 128)], left_out.at[r, q])

    for d in range(3):
        for r in range(4):
            arrived(pairs.at[y, :, pl.ds(128 * r, 128)], pair_out.at[d, r])
    for s in range(3):
        arrived(chain.at[s, h], chain_out.at[s])
    for order in range(2):
        arrived(ends.at[xh, :, 0], ends_out.at[order])

    def level_sent(level, carry):
        for order in range(2):
            for d in range(3):
                arrived(gathered.at[level, :, 0, y], gather_out.at[level, order, d])
        return carry

    lax.fori_loop(0, WIDE + 3, level_sent, 0)

    def shift_sent(level, carry):
        arrived(period.at[level], shift_out.at[level])
        return carry

    lax.fori_loop(0, WIDE, shift_sent, 0)

    def sibling_sent(level, carry):
        arrived(sibling.at[level], sib_out.at[level])
        return carry

    lax.fori_loop(0, WIDE + 1, sibling_sent, 0)
    for n in range(5):
        arrived(late.at[0], late_out.at[n])

    def scatter_sent(j, carry):
        for core in range(2):
            @pl.when(jnp.logical_not((16 * h + j == c) & (h == core)))
            def _():
                arrived(tiles.at[core, j], all_out.at[core, j])
        return carry

    lax.fori_loop(0, 16, scatter_sent, 0)
    arrived(landed, all_sem)
    o_ref[...] = landed[...]


def per_device(steps):
    dma = pltpu.SemaphoreType.DMA
    landed = pl.pallas_call(
        kernel,
        out_shape=jax.ShapeDtypeStruct((32, 16, 128), BF16),
        in_specs=[pl.BlockSpec(memory_space=pl.ANY)],
        out_specs=pl.BlockSpec(memory_space=pltpu.VMEM),
        scratch_shapes=[
            pltpu.VMEM((2, 2, 512, 256), BF16),
            pltpu.VMEM((2, 512, 256), BF16),
            pltpu.VMEM((4, 2, 512, 256), BF16),
            pltpu.VMEM((2, 512, 256), BF16),
            pltpu.VMEM((3, 2, 2, 2, 2, 64, 256), BF16),
            pltpu.VMEM((2, 256, 256), F32),
            pltpu.VMEM((2, 2, 2, 64, 256), BF16),
            pltpu.VMEM((WIDE + 1, 2, 2, 64, 256), BF16),
            pltpu.VMEM((WIDE, 2, 2, 64, 256), BF16),
            pltpu.VMEM((WIDE + 3, 2, 2, 4, 64, 256), BF16),
            pltpu.VMEM((WIDE + 1, 2, 2, 64, 256), BF16),
            pltpu.VMEM((2, 2, 64, 256), BF16),
            pltpu.VMEM((2, 2, 64, 256), BF16),
            pltpu.VMEM((2, 2, 64, 256), BF16),
            pltpu.VMEM((2, 16, 16, 128), BF16),
            pltpu.VMEM((32, 16, 128), BF16),
            dma((4, 2)), dma, dma((4, 2)), dma,
            dma((3, 4)), dma((3, 4)), dma((3,)), dma((3,)),
            dma((2,)), dma((2,)), dma((WIDE + 1,)), dma((WIDE + 1,)),
            dma((WIDE,)), dma((WIDE,)), dma((WIDE + 3, 2, 3)), dma((WIDE + 3, 2, 3)),
            dma((5,)), dma((5,)), dma, dma((2, 16)),
        ],
        compiler_params=pltpu.CompilerParams(
            collective_id=0, has_side_effects=True, vmem_limit_bytes=60 * 1024 * 1024
        ),
        cost_estimate=pl.CostEstimate(
            flops=8 * 512 * 512 * 512 * 3, bytes_accessed=4 * 1024 * 1024, transcendentals=0
        ),
        name="propagate",
    )(steps)
    count = 32
    index = jnp.arange(count, dtype=jnp.int32)
    angle = 2.0 * math.pi / count * (index[:, None] * index[None, :] % count).astype(F32)
    cosine, sine = jnp.cos(angle), jnp.sin(angle)
    values = landed.astype(F32)
    real_in = values[:, :, :32].reshape(count, 512)
    imag_in = values[:, :, 32:64].reshape(count, 512)
    hp = lax.Precision.HIGHEST
    real = jnp.dot(cosine, real_in, precision=hp) + jnp.dot(sine, imag_in, precision=hp)
    imag = jnp.dot(cosine, imag_in, precision=hp) - jnp.dot(sine, real_in, precision=hp)
    result = jnp.stack([real, imag], axis=1) * math.sqrt(512 / count)
    return result.reshape(count, 2, 16, 32).transpose(0, 1, 3, 2)


def solution(mesh):
    return jax.shard_map(
        per_device,
        mesh=mesh,
        in_specs=(P(("cuts", "blk"), None, None, None),),
        out_specs=P(None, None, "blk", "cuts"),
        check_vma=False,
    )
```

```python
import math

import jax
import jax.numpy as jnp
from jax import lax
from jax.experimental import pallas as pl
from jax.experimental.pallas import tpu as pltpu
from jax.sharding import PartitionSpec as P

MESH = pl.DeviceIdType.MESH
F32 = jnp.float32
BF16 = jnp.bfloat16
LEVELS = 5
WIDE = 3


def dot(a, b):
    return jnp.dot(a, b, preferred_element_type=F32)


def arrived(ref, sem):
    pltpu.make_async_copy(ref, ref, sem).wait()


def send(src, dst, send_sem, recv_sem, device):
    pltpu.make_async_remote_copy(
        src_ref=src,
        dst_ref=dst,
        send_sem=send_sem,
        recv_sem=recv_sem,
        device_id=device,
        device_id_type=MESH,
    ).start()


def combine(by_real, by_imag):
    rows = by_real.shape[0] // 2
    return by_real[:rows] - by_imag[rows:], by_imag[:rows] + by_real[rows:]


def halves(value):
    high = value.astype(BF16)
    return high, (value - high.astype(F32)).astype(BF16)


def kernel(
    x_ref, o_ref,
    left, right, pairs, pair_low, chain, acc, ends, sibling, shifted, gathered, period,
    late_shift, late_sib, late, tiles, landed,
    left_sem, right_sem, left_out, right_out, pair_sem, pair_out, first_sem, first_out, chain_sem, chain_out,
    ends_sem, ends_out, sib_sem, sib_out, shift_sem, shift_out, gather_sem, gather_out,
    late_sem, late_out, all_sem, all_out,
):
    c = lax.axis_index("cuts")
    b = lax.axis_index("blk")
    xh = lax.div(b, 8)
    y = lax.rem(lax.div(b, 2), 4)
    h = lax.rem(b, 2)
    other = 1 - h
    sib = (c, b + 1 - 2 * h)
    opposite = (c, b + 8 - 16 * xh)

    def along_y(d):
        return (c, xh * 8 + lax.rem(y + d, 4) * 2 + h)

    def cut(k):
        return (lax.rem(c + k + 32, 32), b)

    @pl.when(h == 0)
    def _():
        pltpu.make_async_copy(x_ref.at[0, :, :, pl.ds(0, 256)], right, right_sem).start()

    @pl.when(h == 1)
    def _():
        for r in range(4):
            for q in range(2):
                pltpu.make_async_copy(
                    x_ref.at[0, :, pl.ds(128 * r, 128), pl.ds(256 * q, 256)],
                    left.at[q, :, pl.ds(128 * r, 128)],
                    left_sem.at[r, q],
                ).start()

    barrier = pltpu.get_barrier_semaphore()
    greet = [sib, opposite] + [along_y(d) for d in (1, 2, 3)] + [cut(1 << s) for s in range(LEVELS)]
    for device in greet:
        pl.semaphore_signal(barrier, inc=1, device_id=device, device_id_type=MESH)
    pl.semaphore_wait(barrier, len(greet))

    @pl.when(h == 0)
    def _():
        send(x_ref.at[0, :, :, pl.ds(256, 256)], right, right_out, right_sem, sib)

    @pl.when(h == 1)
    def _():
        for r in range(4):
            for q in range(2):
                send(
                    x_ref.at[0, :, pl.ds(128 * r, 128), pl.ds(256 * q, 256)],
                    left.at[q, :, pl.ds(128 * r, 128)],
                    left_out.at[r, q],
                    left_sem.at[r, q],
                    sib,
                )

    arrived(right, right_sem)

    def pass_pair(r, d):
        block = pairs.at[y, :, pl.ds(pl.multiple_of(128 * r, 128), 128)]
        send(block, block, pair_out.at[d - 1, r], pair_sem.at[d - 1, r], along_y(d))

    def pair_chunk(r, carry):
        rows = pl.ds(pl.multiple_of(128 * r, 128), 128)
        for q in range(2):
            arrived(left.at[q, :, rows], left_sem.at[r, q])
        x0 = left[0, :, rows, :].reshape(256, 256)
        x1 = left[1, :, rows, :].reshape(256, 256)
        by = [dot(x0, right[i, :256]) + dot(x1, right[i, 256:]) for i in range(2)]
        for i, part in enumerate(combine(*by)):
            high, low = halves(part)
            pairs[y, i, rows, :] = high
            pair_low[i, rows, :] = low

        @pl.when(y != 3)
        def _():
            pass_pair(r, 1 + 2 * lax.rem(r, 2))

        @pl.when(y == 3)
        def _():
            p = lax.div(r, 2)
            for n in range(2):
                chip = 2 * lax.rem(r, 2) + n
                part = pl.ds(pl.multiple_of(128 * r + 64 * n, 64), 64)

                @pl.when(chip != 3)
                def _():
                    for low, src in enumerate((pairs.at[3, :, part], pair_low.at[:, part])):
                        send(
                            src, chain.at[0, h, low, :, p],
                            first_out.at[chip, low, p], first_sem.at[low, p],
                            (c, xh * 8 + chip * 2 + h),
                        )

        return carry

    lax.fori_loop(0, 4, pair_chunk, 0)

    for r in range(4):
        d = 1 if r % 2 == 0 else 3

        @pl.when(y != (0 if d == 1 else 2))
        def _():
            block = pairs.at[lax.rem(y + 4 - d, 4), :, pl.ds(128 * r, 128)]
            arrived(block, pair_sem.at[d - 1, r])
            send(block, block, pair_out.at[1, r], pair_sem.at[1, r], along_y(d))

        @pl.when(y != 3)
        def _():
            pass_pair(r, 4 - d)

    def wait_pair(j):
        for d, chunks in ((1, (1, 3)), (2, (0, 1, 2, 3)), (3, (0, 2))):
            @pl.when(lax.rem(y - j + 4, 4) == d)
            def _():
                for r in chunks:
                    arrived(pairs.at[j, :, pl.ds(128 * r, 128)], pair_sem.at[d - 1, r])

    def exchange_chain(s):
        send(chain.at[s, h], chain.at[s, h], chain_out.at[s], chain_sem.at[s], sib)

    @pl.when(y == 3)
    def _():
        for p in range(2):
            rows = pl.ds(256 * p + 192, 64)
            chain[0, h, 0, :, p] = pairs[3, :, rows, :]
            chain[0, h, 1, :, p] = pair_low[:, rows, :]

    @pl.when(y != 3)
    def _():
        for low in range(2):
            for p in range(2):
                arrived(chain.at[0, h, low, :, p], first_sem.at[low, p])

    exchange_chain(0)
    for s in range(3):
        j = 2 - s
        wait_pair(j)
        arrived(chain.at[s, other], chain_sem.at[s])
        x0 = chain[s, 0].reshape(512, 256)
        x1 = chain[s, 1].reshape(512, 256)
        for i in range(2):
            t = dot(x0, pairs[j, i, :256]) + dot(x1, pairs[j, i, 256:])
            acc[i] = t[:256] + t[256:]

        @pl.when(y == j)
        def _():
            for i in range(2):
                acc[i] += dot(x0[:256], pair_low[i, :256]) + dot(x1[:256], pair_low[i, 256:])

        for i, part in enumerate(combine(acc[0], acc[1])):
            part = part.reshape(2, 64, 256)
            if s < 2:
                chain[s + 1, h, 0, i], chain[s + 1, h, 1, i] = halves(part)
            else:
                ends[xh, i] = part.astype(BF16)
        if s < 2:
            exchange_chain(s + 1)

    def spread(src, level, order, p):
        for d in (1, 3, 2):
            send(
                src, gathered.at[level, :, p, y],
                gather_out.at[level, order, d - 1], gather_sem.at[level, order, d - 1], along_y(d),
            )

    def spread_arrived(level, order, p):
        for d in (1, 2, 3):
            arrived(gathered.at[level, :, p, lax.rem(y - d + 4, 4)], gather_sem.at[level, order, d - 1])

    def half_product(x, level, p):
        return [dot(x, gathered[level, i, p].reshape(256, 256)) for i in range(2)]

    def product(own, theirs, theirs_sem, level):
        rows = 2 * math.prod(own.shape[1:-1])
        spread_arrived(level, 0, h)
        by = half_product(own[...].reshape(rows, 256), level, h)
        arrived(theirs, theirs_sem)
        spread_arrived(level, 1, other)
        more = half_product(theirs[...].reshape(rows, 256), level, other)
        return combine(by[0] + more[0], by[1] + more[1])

    def keep(parts, level):
        for i, part in enumerate(parts):
            part = part.reshape(2, 64, 256).astype(BF16)
            period[level, i] = part
            gathered[level + 1, i, :, y] = part

    for order, p in enumerate((h, other)):
        send(ends.at[xh, :, p], ends.at[xh, :, p], ends_out.at[order], ends_sem.at[order], opposite)
    for order, p in enumerate((h, other)):
        arrived(ends.at[1 - xh, :, p], ends_sem.at[order])
        spread(ends.at[0, :, p], 0, order, p)
    send(ends.at[1], sibling.at[0], sib_out.at[0], sib_sem.at[0], sib)
    gathered[0, :, :, y] = ends[0]
    keep(product(ends.at[1], sibling.at[0], sib_sem.at[0], 0), 0)

    def double(level, k):
        send(period.at[level], shifted.at[level], shift_out.at[level], shift_sem.at[level], cut(-k))
        for order, p in enumerate((h, other)):
            spread(period.at[level, :, p], level + 1, order, p)
        arrived(shifted.at[level], shift_sem.at[level])
        after = level + 1
        send(shifted.at[level], sibling.at[after], sib_out.at[after], sib_sem.at[after], sib)
        keep(product(shifted.at[level], sibling.at[after], sib_sem.at[after], after), after)
        return 2 * k

    lax.fori_loop(0, WIDE, double, jnp.int32(1))

    send(period.at[WIDE, :, xh], late_shift.at[0], late_out.at[0], late_sem.at[0], cut(-8))
    for order, p in enumerate((h, other)):
        spread(period.at[WIDE, :, p], WIDE + 1, order, p)
    arrived(late_shift.at[0], late_sem.at[0])
    send(late_shift.at[0], late_sib.at[0], late_out.at[1], late_sem.at[1], sib)
    for i, part in enumerate(product(late_shift.at[0], late_sib.at[0], late_sem.at[1], WIDE + 1)):
        part = part.astype(BF16)
        late[0, i] = part
        gathered[WIDE + 2, i, xh, y] = part

    send(late.at[0], late_shift.at[1], late_out.at[2], late_sem.at[2], cut(-16))
    send(late.at[0], late.at[1], late_out.at[3], late_sem.at[3], opposite)
    level = WIDE + 2
    spread(late.at[0], level, lax.rem(xh + h, 2), xh)
    arrived(late.at[1], late_sem.at[3])
    spread(late.at[1], level, lax.rem(1 - xh + h, 2), 1 - xh)
    gathered[level, :, 1 - xh, y] = late[1]
    arrived(late_shift.at[1], late_sem.at[2])
    send(late_shift.at[1], late_sib.at[1], late_out.at[4], late_sem.at[4], sib)
    real, imag = product(late_shift.at[1], late_sib.at[1], late_sem.at[4], level)

    stacked = jnp.concatenate([real[:32], imag[:32], real[32:], imag[32:]], axis=0)
    turned = stacked.T
    tiles[0] = turned.astype(BF16).reshape(16, 16, 128)
    turned = jnp.concatenate([turned[:, 64:], turned[:, :64]], axis=1)
    tiles[1] = turned.astype(BF16).reshape(16, 16, 128)
    same = lax.div(c, 16) == h

    def nearness(t):
        t = jnp.where(same, 15 - t, t)
        step = lax.div(t + 1, 2)
        return lax.rem(c + jnp.where(lax.rem(t, 2) == 1, step, 16 - step), 16)

    def scatter(t, carry):
        j = nearness(t)
        target = 16 * h + j
        for core in range(2):
            here = (target == c) & (h == core)

            @pl.when(here)
            def _():
                pltpu.make_async_copy(tiles.at[core, j], landed.at[c], all_sem).start()

            @pl.when(jnp.logical_not(here))
            def _():
                send(
                    tiles.at[core, j], landed.at[c], all_out.at[core, j], all_sem,
                    (target, xh * 8 + y * 2 + core),
                )
        return carry

    lax.fori_loop(0, 16, scatter, 0)

    @pl.when(h == 0)
    def _():
        arrived(right, right_out)

    @pl.when(h == 1)
    def _():
        for r in range(4):
            for q in range(2):
                arrived(left.at[q, :, pl.ds(128 * r, 128)], left_out.at[r, q])

    @pl.when(y != 3)
    def _():
        for d in (1, 3):
            for r in range(4):
                arrived(pairs.at[y, :, pl.ds(128 * r, 128)], pair_out.at[d - 1, r])

    @pl.when(y == 3)
    def _():
        for chip in range(3):
            for low in range(2):
                for p in range(2):
                    arrived(pair_low.at[:, pl.ds(0, 64)], first_out.at[chip, low, p])

    for r in range(4):
        @pl.when(y != (0 if r % 2 == 0 else 2))
        def _():
            arrived(pairs.at[y, :, pl.ds(128 * r, 128)], pair_out.at[1, r])

    for s in range(3):
        arrived(chain.at[s, h], chain_out.at[s])
    for order in range(2):
        arrived(ends.at[xh, :, 0], ends_out.at[order])

    def level_sent(level, carry):
        for order in range(2):
            for d in range(3):
                arrived(gathered.at[level, :, 0, y], gather_out.at[level, order, d])
        return carry

    lax.fori_loop(0, WIDE + 3, level_sent, 0)

    def shift_sent(level, carry):
        arrived(period.at[level], shift_out.at[level])
        return carry

    lax.fori_loop(0, WIDE, shift_sent, 0)

    def sibling_sent(level, carry):
        arrived(sibling.at[level], sib_out.at[level])
        return carry

    lax.fori_loop(0, WIDE + 1, sibling_sent, 0)
    for n in range(5):
        arrived(late.at[0], late_out.at[n])

    def scatter_sent(j, carry):
        for core in range(2):
            @pl.when(jnp.logical_not((16 * h + j == c) & (h == core)))
            def _():
                arrived(tiles.at[core, j], all_out.at[core, j])
        return carry

    lax.fori_loop(0, 16, scatter_sent, 0)
    arrived(landed, all_sem)
    o_ref[...] = landed[...]


def per_device(steps):
    dma = pltpu.SemaphoreType.DMA
    landed = pl.pallas_call(
        kernel,
        out_shape=jax.ShapeDtypeStruct((32, 16, 128), BF16),
        in_specs=[pl.BlockSpec(memory_space=pl.ANY)],
        out_specs=pl.BlockSpec(memory_space=pltpu.VMEM),
        scratch_shapes=[
            pltpu.VMEM((2, 2, 512, 256), BF16),
            pltpu.VMEM((2, 512, 256), BF16),
            pltpu.VMEM((4, 2, 512, 256), BF16),
            pltpu.VMEM((2, 512, 256), BF16),
            pltpu.VMEM((3, 2, 2, 2, 2, 64, 256), BF16),
            pltpu.VMEM((2, 256, 256), F32),
            pltpu.VMEM((2, 2, 2, 64, 256), BF16),
            pltpu.VMEM((WIDE + 1, 2, 2, 64, 256), BF16),
            pltpu.VMEM((WIDE, 2, 2, 64, 256), BF16),
            pltpu.VMEM((WIDE + 3, 2, 2, 4, 64, 256), BF16),
            pltpu.VMEM((WIDE + 1, 2, 2, 64, 256), BF16),
            pltpu.VMEM((2, 2, 64, 256), BF16),
            pltpu.VMEM((2, 2, 64, 256), BF16),
            pltpu.VMEM((2, 2, 64, 256), BF16),
            pltpu.VMEM((2, 16, 16, 128), BF16),
            pltpu.VMEM((32, 16, 128), BF16),
            dma((4, 2)), dma, dma((4, 2)), dma,
            dma((3, 4)), dma((3, 4)), dma((2, 2)), dma((3, 2, 2)), dma((3,)), dma((3,)),
            dma((2,)), dma((2,)), dma((WIDE + 1,)), dma((WIDE + 1,)),
            dma((WIDE,)), dma((WIDE,)), dma((WIDE + 3, 2, 3)), dma((WIDE + 3, 2, 3)),
            dma((5,)), dma((5,)), dma, dma((2, 16)),
        ],
        compiler_params=pltpu.CompilerParams(
            collective_id=0, has_side_effects=True, vmem_limit_bytes=60 * 1024 * 1024
        ),
        cost_estimate=pl.CostEstimate(
            flops=8 * 512 * 512 * 512 * 3, bytes_accessed=4 * 1024 * 1024, transcendentals=0
        ),
        name="propagate",
    )(steps)
    count = 32
    index = jnp.arange(count, dtype=jnp.int32)
    angle = 2.0 * math.pi / count * (index[:, None] * index[None, :] % count).astype(F32)
    cosine, sine = jnp.cos(angle), jnp.sin(angle)
    values = landed.astype(F32)
    real_in = values[:, :, :32].reshape(count, 512)
    imag_in = values[:, :, 32:64].reshape(count, 512)
    hp = lax.Precision.HIGHEST
    real = jnp.dot(cosine, real_in, precision=hp) + jnp.dot(sine, imag_in, precision=hp)
    imag = jnp.dot(cosine, imag_in, precision=hp) - jnp.dot(sine, real_in, precision=hp)
    result = jnp.stack([real, imag], axis=1) * math.sqrt(512 / count)
    return result.reshape(count, 2, 16, 32).transpose(0, 1, 3, 2)


def solution(mesh):
    return jax.shard_map(
        per_device,
        mesh=mesh,
        in_specs=(P(("cuts", "blk"), None, None, None),),
        out_specs=P(None, None, "blk", "cuts"),
        check_vma=False,
    )
```

```python
import math

import jax
import jax.numpy as jnp
from jax import lax
from jax.experimental import pallas as pl
from jax.experimental.pallas import tpu as pltpu
from jax.sharding import PartitionSpec as P

MESH = pl.DeviceIdType.MESH
F32 = jnp.float32
BF16 = jnp.bfloat16
LEVELS = 5
WIDE = 3


def dot(a, b):
    return jnp.dot(a, b, preferred_element_type=F32)


def arrived(ref, sem):
    pltpu.make_async_copy(ref, ref, sem).wait()


def send(src, dst, send_sem, recv_sem, device):
    pltpu.make_async_remote_copy(
        src_ref=src,
        dst_ref=dst,
        send_sem=send_sem,
        recv_sem=recv_sem,
        device_id=device,
        device_id_type=MESH,
    ).start()


def combine(by_real, by_imag):
    rows = by_real.shape[0] // 2
    return by_real[:rows] - by_imag[rows:], by_imag[:rows] + by_real[rows:]


def halves(value):
    high = value.astype(BF16)
    return high, (value - high.astype(F32)).astype(BF16)


def kernel(
    x_ref, o_ref,
    left, right, pairs, pair_low, chain, acc, end_left, end_right, end_sib,
    sibling, shifted, gathered, period, beside, turn, turn_sib, cross,
    late_shift, late_sib, late, final, tiles, landed,
    left_sem, right_sem, left_out, right_out, pair_sem, pair_out, first_sem, first_out, chain_sem, chain_out,
    ends_sem, ends_out, end_sib_sem, end_sib_out, sib_sem, sib_out, shift_sem, shift_out, gather_sem, gather_out,
    turn_sem, turn_out, late_sem, late_out, final_sem, final_out, all_sem, all_out,
):
    c = lax.axis_index("cuts")
    b = lax.axis_index("blk")
    xh = lax.div(b, 8)
    y = lax.rem(lax.div(b, 2), 4)
    h = lax.rem(b, 2)
    other = 1 - h
    sib = (c, b + 1 - 2 * h)
    opposite = (c, b + 8 - 16 * xh)

    def along_y(d):
        return (c, xh * 8 + lax.rem(y + d, 4) * 2 + h)

    def cut(k):
        return (lax.rem(c + k + 32, 32), b)

    def cut_over(k):
        return (lax.rem(c + k + 32, 32), opposite[1])

    @pl.when(h == 0)
    def _():
        pltpu.make_async_copy(x_ref.at[0, :, :, pl.ds(0, 256)], right, right_sem).start()

    @pl.when(h == 1)
    def _():
        for r in range(4):
            for q in range(2):
                pltpu.make_async_copy(
                    x_ref.at[0, :, pl.ds(128 * r, 128), pl.ds(256 * q, 256)],
                    left.at[q, :, pl.ds(128 * r, 128)],
                    left_sem.at[r, q],
                ).start()

    barrier = pltpu.get_barrier_semaphore()
    greet = [sib, opposite] + [along_y(d) for d in (1, 2, 3)] + [cut(1 << s) for s in range(LEVELS)]
    greet += [cut_over(1 << s) for s in range(WIDE + 1)]
    for device in greet:
        pl.semaphore_signal(barrier, inc=1, device_id=device, device_id_type=MESH)
    pl.semaphore_wait(barrier, len(greet))

    @pl.when(h == 0)
    def _():
        send(x_ref.at[0, :, :, pl.ds(256, 256)], right, right_out, right_sem, sib)

    @pl.when(h == 1)
    def _():
        for r in range(4):
            for q in range(2):
                send(
                    x_ref.at[0, :, pl.ds(128 * r, 128), pl.ds(256 * q, 256)],
                    left.at[q, :, pl.ds(128 * r, 128)],
                    left_out.at[r, q],
                    left_sem.at[r, q],
                    sib,
                )

    arrived(right, right_sem)

    def pass_pair(r, d):
        block = pairs.at[y, :, pl.ds(pl.multiple_of(128 * r, 128), 128)]
        send(block, block, pair_out.at[d - 1, r], pair_sem.at[d - 1, r], along_y(d))

    def pair_chunk(r, carry):
        rows = pl.ds(pl.multiple_of(128 * r, 128), 128)
        for q in range(2):
            arrived(left.at[q, :, rows], left_sem.at[r, q])
        x0 = left[0, :, rows, :].reshape(256, 256)
        x1 = left[1, :, rows, :].reshape(256, 256)
        by = [dot(x0, right[i, :256]) + dot(x1, right[i, 256:]) for i in range(2)]
        for i, part in enumerate(combine(*by)):
            high, low = halves(part)
            pairs[y, i, rows, :] = high
            pair_low[i, rows, :] = low

        @pl.when(y != 3)
        def _():
            pass_pair(r, 1 + 2 * lax.rem(r, 2))

        @pl.when(y == 3)
        def _():
            p = lax.div(r, 2)
            for n in range(2):
                chip = 2 * lax.rem(r, 2) + n
                part = pl.ds(pl.multiple_of(128 * r + 64 * n, 64), 64)

                @pl.when(chip != 3)
                def _():
                    for low, src in enumerate((pairs.at[3, :, part], pair_low.at[:, part])):
                        send(
                            src, chain.at[0, h, low, :, p],
                            first_out.at[chip, low, p], first_sem.at[low, p],
                            (c, xh * 8 + chip * 2 + h),
                        )

        return carry

    lax.fori_loop(0, 4, pair_chunk, 0)

    for r in range(4):
        d = 1 if r % 2 == 0 else 3

        @pl.when(y != (0 if d == 1 else 2))
        def _():
            block = pairs.at[lax.rem(y + 4 - d, 4), :, pl.ds(128 * r, 128)]
            arrived(block, pair_sem.at[d - 1, r])
            send(block, block, pair_out.at[1, r], pair_sem.at[1, r], along_y(d))

        @pl.when(y != 3)
        def _():
            pass_pair(r, 4 - d)

    def wait_pair(j):
        for d, chunks in ((1, (1, 3)), (2, (0, 1, 2, 3)), (3, (0, 2))):
            @pl.when(lax.rem(y - j + 4, 4) == d)
            def _():
                for r in chunks:
                    arrived(pairs.at[j, :, pl.ds(128 * r, 128)], pair_sem.at[d - 1, r])

    def exchange_chain(s):
        send(chain.at[s, h], chain.at[s, h], chain_out.at[s], chain_sem.at[s], sib)

    @pl.when(y == 3)
    def _():
        for p in range(2):
            rows = pl.ds(256 * p + 192, 64)
            chain[0, h, 0, :, p] = pairs[3, :, rows, :]
            chain[0, h, 1, :, p] = pair_low[:, rows, :]

    @pl.when(y != 3)
    def _():
        for low in range(2):
            for p in range(2):
                arrived(chain.at[0, h, low, :, p], first_sem.at[low, p])

    exchange_chain(0)
    ends = []
    for s in range(3):
        j = 2 - s
        wait_pair(j)
        arrived(chain.at[s, other], chain_sem.at[s])
        x0 = chain[s, 0].reshape(512, 256)
        x1 = chain[s, 1].reshape(512, 256)
        for i in range(2):
            t = dot(x0, pairs[j, i, :256]) + dot(x1, pairs[j, i, 256:])
            acc[i] = t[:256] + t[256:]

        @pl.when(y == j)
        def _():
            for i in range(2):
                acc[i] += dot(x0[:256], pair_low[i, :256]) + dot(x1[:256], pair_low[i, 256:])

        for i, part in enumerate(combine(acc[0], acc[1])):
            part = part.reshape(2, 64, 256)
            if s < 2:
                chain[s + 1, h, 0, i], chain[s + 1, h, 1, i] = halves(part)
            else:
                ends.append(part.astype(BF16))
        if s < 2:
            exchange_chain(s + 1)

    @pl.when(xh == 0)
    def _():
        for q in range(2):
            end_right[q] = jnp.concatenate([part[:, :, 128 * q : 128 * q + 128] for part in ends], axis=2)

    @pl.when(xh == 1)
    def _():
        for i in range(2):
            end_left[i] = ends[i]

    def spread(src, level):
        for d in (1, 3, 2):
            send(
                src, gathered.at[level, :, y],
                gather_out.at[level, d - 1], gather_sem.at[level, d - 1], along_y(d),
            )

    def spread_arrived(level):
        for d in (1, 2, 3):
            arrived(gathered.at[level, :, lax.rem(y - d + 4, 4)], gather_sem.at[level, d - 1])

    def quarter_product(x, level, p):
        return dot(x, gathered[level, p].reshape(256, 256))

    def quarter(t):
        rows = t.shape[0] // 2
        return t[:rows, :128] - t[rows:, 128:], t[:rows, 128:] + t[rows:, :128]

    def joined(blocks):
        rows = math.prod(blocks.shape[1:-1])
        return jnp.concatenate([blocks[0].reshape(rows, 128), blocks[1].reshape(rows, 128)], axis=1)

    def keep(t, level):
        parts = [part.reshape(2, 64, 128).astype(BF16) for part in quarter(t)]
        for i in range(2):
            period[level, i] = parts[i]
        side = jnp.concatenate(parts, axis=2)
        beside[level] = side
        gathered[level + 1, :, y] = side

    @pl.when(xh == 0)
    def _():
        send(end_right.at[1], end_right.at[0], ends_out, ends_sem, opposite)

    @pl.when(xh == 1)
    def _():
        send(end_left, end_left, ends_out, ends_sem, opposite)
        arrived(end_right.at[0], ends_sem)

    spread(end_right.at[0], 0)
    gathered[0, :, y] = end_right[0]

    @pl.when(xh == 0)
    def _():
        arrived(end_left, ends_sem)

    send(end_left, end_sib, end_sib_out, end_sib_sem, sib)
    spread_arrived(0)
    t = quarter_product(end_left[...].reshape(256, 256), 0, h)
    arrived(end_sib, end_sib_sem)
    keep(t + quarter_product(end_sib[...].reshape(256, 256), 0, other), 0)

    def double(level, k):
        for n, device in enumerate((cut(-k), cut_over(-k))):
            send(
                period.at[level], shifted.at[level, xh],
                shift_out.at[level, n], shift_sem.at[level, xh], device,
            )
        spread(beside.at[level], level + 1)
        for q in (xh, 1 - xh):
            arrived(shifted.at[level, q], shift_sem.at[level, q])
            send(
                shifted.at[level, q], sibling.at[level, q],
                sib_out.at[level, q], sib_sem.at[level, q], sib,
            )
        spread_arrived(level + 1)
        t = quarter_product(joined(shifted.at[level]), level + 1, h)
        for q in range(2):
            arrived(sibling.at[level, q], sib_sem.at[level, q])
        keep(t + quarter_product(joined(sibling.at[level]), level + 1, other), level + 1)
        return 2 * k

    lax.fori_loop(0, WIDE, double, jnp.int32(1))

    for half in range(2):
        send(
            period.at[WIDE, :, half], turn.at[xh], turn_out.at[half], turn_sem.at[xh],
            (lax.rem(c + 24, 32), half * 8 + y * 2 + h),
        )
    send(beside.at[WIDE], cross, late_out.at[0], late_sem.at[0], opposite)
    spread(beside.at[WIDE], WIDE + 1)
    arrived(cross, late_sem.at[0])
    spread(cross, WIDE + 2)
    gathered[WIDE + 2, :, y] = cross[...]
    for q in range(2):
        arrived(turn.at[q], turn_sem.at[q])
    send(turn, turn_sib, late_out.at[1], late_sem.at[1], sib)
    x0 = joined(turn)
    spread_arrived(WIDE + 1)
    own = quarter_product(x0, WIDE + 1, h)
    arrived(turn_sib, late_sem.at[1])
    x1 = joined(turn_sib)
    own = quarter(own + quarter_product(x1, WIDE + 1, other))
    spread_arrived(WIDE + 2)
    far = quarter(quarter_product(x0, WIDE + 2, h) + quarter_product(x1, WIDE + 2, other))
    for i in range(2):
        first = jnp.where(xh == 0, own[i], far[i])
        second = jnp.where(xh == 0, far[i], own[i])
        part = jnp.concatenate([first, second], axis=1).astype(BF16)
        late[0, i] = part
        final[i, xh, y] = part

    def spread_final(src, p, order):
        for d in (1, 3, 2):
            send(
                src, final.at[:, p, y],
                final_out.at[order, d - 1], final_sem.at[order, d - 1], along_y(d),
            )

    send(late.at[0], late_shift, late_out.at[2], late_sem.at[2], cut(-16))
    send(late.at[0], late.at[1], late_out.at[3], late_sem.at[3], opposite)
    spread_final(late.at[0], xh, 0)
    arrived(late.at[1], late_sem.at[3])
    spread_final(late.at[1], 1 - xh, 1)
    final[:, 1 - xh, y] = late[1]
    arrived(late_shift, late_sem.at[2])
    send(late_shift, late_sib, late_out.at[4], late_sem.at[4], sib)
    for order, p in enumerate((xh, 1 - xh)):
        for d in (1, 2, 3):
            arrived(final.at[:, p, lax.rem(y - d + 4, 4)], final_sem.at[order, d - 1])
    x0 = late_shift[...].reshape(128, 256)
    by = [dot(x0, final[i, h].reshape(256, 256)) for i in range(2)]
    arrived(late_sib, late_sem.at[4])
    x1 = late_sib[...].reshape(128, 256)
    by = [by[i] + dot(x1, final[i, other].reshape(256, 256)) for i in range(2)]
    real, imag = combine(*by)

    stacked = jnp.concatenate([real[:32], imag[:32], real[32:], imag[32:]], axis=0)
    turned = stacked.T
    tiles[0] = turned.astype(BF16).reshape(16, 16, 128)
    turned = jnp.concatenate([turned[:, 64:], turned[:, :64]], axis=1)
    tiles[1] = turned.astype(BF16).reshape(16, 16, 128)
    same = lax.div(c, 16) == h

    def nearness(t):
        t = jnp.where(same, 15 - t, t)
        step = lax.div(t + 1, 2)
        return lax.rem(c + jnp.where(lax.rem(t, 2) == 1, step, 16 - step), 16)

    def scatter(t, carry):
        j = nearness(t)
        target = 16 * h + j
        for core in range(2):
            here = (target == c) & (h == core)

            @pl.when(here)
            def _():
                pltpu.make_async_copy(tiles.at[core, j], landed.at[c], all_sem).start()

            @pl.when(jnp.logical_not(here))
            def _():
                send(
                    tiles.at[core, j], landed.at[c], all_out.at[core, j], all_sem,
                    (target, xh * 8 + y * 2 + core),
                )
        return carry

    lax.fori_loop(0, 16, scatter, 0)

    @pl.when(h == 0)
    def _():
        arrived(right, right_out)

    @pl.when(h == 1)
    def _():
        for r in range(4):
            for q in range(2):
                arrived(left.at[q, :, pl.ds(128 * r, 128)], left_out.at[r, q])

    @pl.when(y != 3)
    def _():
        for d in (1, 3):
            for r in range(4):
                arrived(pairs.at[y, :, pl.ds(128 * r, 128)], pair_out.at[d - 1, r])

    @pl.when(y == 3)
    def _():
        for chip in range(3):
            for low in range(2):
                for p in range(2):
                    arrived(pair_low.at[:, pl.ds(0, 64)], first_out.at[chip, low, p])

    for r in range(4):
        @pl.when(y != (0 if r % 2 == 0 else 2))
        def _():
            arrived(pairs.at[y, :, pl.ds(128 * r, 128)], pair_out.at[1, r])

    for s in range(3):
        arrived(chain.at[s, h], chain_out.at[s])
    @pl.when(xh == 0)
    def _():
        arrived(end_right.at[1], ends_out)

    @pl.when(xh == 1)
    def _():
        arrived(end_left, ends_out)

    arrived(end_sib, end_sib_out)

    def level_sent(level, carry):
        for d in range(3):
            arrived(gathered.at[level, :, y], gather_out.at[level, d])
        return carry

    lax.fori_loop(0, WIDE + 3, level_sent, 0)

    def shift_sent(level, carry):
        for n in range(2):
            arrived(period.at[level], shift_out.at[level, n])
            arrived(sibling.at[level, n], sib_out.at[level, n])
        return carry

    lax.fori_loop(0, WIDE, shift_sent, 0)
    for half in range(2):
        arrived(turn.at[half], turn_out.at[half])
    for n in range(5):
        arrived(cross if n == 0 else late.at[0], late_out.at[n])
    for order in range(2):
        for d in range(3):
            arrived(late.at[0], final_out.at[order, d])

    def scatter_sent(j, carry):
        for core in range(2):
            @pl.when(jnp.logical_not((16 * h + j == c) & (h == core)))
            def _():
                arrived(tiles.at[core, j], all_out.at[core, j])
        return carry

    lax.fori_loop(0, 16, scatter_sent, 0)
    arrived(landed, all_sem)
    o_ref[...] = landed[...]


def per_device(steps):
    dma = pltpu.SemaphoreType.DMA
    landed = pl.pallas_call(
        kernel,
        out_shape=jax.ShapeDtypeStruct((32, 16, 128), BF16),
        in_specs=[pl.BlockSpec(memory_space=pl.ANY)],
        out_specs=pl.BlockSpec(memory_space=pltpu.VMEM),
        scratch_shapes=[
            pltpu.VMEM((2, 2, 512, 256), BF16),
            pltpu.VMEM((2, 512, 256), BF16),
            pltpu.VMEM((4, 2, 512, 256), BF16),
            pltpu.VMEM((2, 512, 256), BF16),
            pltpu.VMEM((3, 2, 2, 2, 2, 64, 256), BF16),
            pltpu.VMEM((2, 256, 256), F32),
            pltpu.VMEM((2, 2, 64, 256), BF16),
            pltpu.VMEM((2, 2, 64, 256), BF16),
            pltpu.VMEM((2, 2, 64, 256), BF16),
            pltpu.VMEM((WIDE, 2, 2, 2, 64, 128), BF16),
            pltpu.VMEM((WIDE, 2, 2, 2, 64, 128), BF16),
            pltpu.VMEM((WIDE + 3, 2, 4, 64, 256), BF16),
            pltpu.VMEM((WIDE + 1, 2, 2, 64, 128), BF16),
            pltpu.VMEM((WIDE + 1, 2, 64, 256), BF16),
            pltpu.VMEM((2, 2, 64, 128), BF16),
            pltpu.VMEM((2, 2, 64, 128), BF16),
            pltpu.VMEM((2, 64, 256), BF16),
            pltpu.VMEM((2, 64, 256), BF16),
            pltpu.VMEM((2, 64, 256), BF16),
            pltpu.VMEM((2, 2, 64, 256), BF16),
            pltpu.VMEM((2, 2, 4, 64, 256), BF16),
            pltpu.VMEM((2, 16, 16, 128), BF16),
            pltpu.VMEM((32, 16, 128), BF16),
            dma((4, 2)), dma, dma((4, 2)), dma,
            dma((3, 4)), dma((3, 4)), dma((2, 2)), dma((3, 2, 2)), dma((3,)), dma((3,)),
            dma, dma, dma, dma, dma((WIDE, 2)), dma((WIDE, 2)),
            dma((WIDE, 2)), dma((WIDE, 2)), dma((WIDE + 3, 3)), dma((WIDE + 3, 3)),
            dma((2,)), dma((2,)), dma((5,)), dma((5,)), dma((2, 3)), dma((2, 3)),
            dma, dma((2, 16)),
        ],
        compiler_params=pltpu.CompilerParams(
            collective_id=0, has_side_effects=True, vmem_limit_bytes=60 * 1024 * 1024
        ),
        cost_estimate=pl.CostEstimate(
            flops=8 * 512 * 512 * 512 * 3, bytes_accessed=4 * 1024 * 1024, transcendentals=0
        ),
        name="propagate",
    )(steps)
    count = 32
    index = jnp.arange(count, dtype=jnp.int32)
    angle = 2.0 * math.pi / count * (index[:, None] * index[None, :] % count).astype(F32)
    cosine, sine = jnp.cos(angle), jnp.sin(angle)
    values = landed.astype(F32)
    real_in = values[:, :, :32].reshape(count, 512)
    imag_in = values[:, :, 32:64].reshape(count, 512)
    hp = lax.Precision.HIGHEST
    real = jnp.dot(cosine, real_in, precision=hp) + jnp.dot(sine, imag_in, precision=hp)
    imag = jnp.dot(cosine, imag_in, precision=hp) - jnp.dot(sine, real_in, precision=hp)
    result = jnp.stack([real, imag], axis=1) * math.sqrt(512 / count)
    return result.reshape(count, 2, 16, 32).transpose(0, 1, 3, 2)


def solution(mesh):
    return jax.shard_map(
        per_device,
        mesh=mesh,
        in_specs=(P(("cuts", "blk"), None, None, None),),
        out_specs=P(None, None, "blk", "cuts"),
        check_vma=False,
    )
```

```python
import math

import jax
import jax.numpy as jnp
from jax import lax
from jax.experimental import pallas as pl
from jax.experimental.pallas import tpu as pltpu
from jax.sharding import PartitionSpec as P

MESH = pl.DeviceIdType.MESH
F32 = jnp.float32
BF16 = jnp.bfloat16
LEVELS = 5
WIDE = 3


def dot(a, b):
    return jnp.dot(a, b, preferred_element_type=F32)


def arrived(ref, sem):
    pltpu.make_async_copy(ref, ref, sem).wait()


def send(src, dst, send_sem, recv_sem, device):
    pltpu.make_async_remote_copy(
        src_ref=src,
        dst_ref=dst,
        send_sem=send_sem,
        recv_sem=recv_sem,
        device_id=device,
        device_id_type=MESH,
    ).start()


def combine(by_real, by_imag):
    rows = by_real.shape[0] // 2
    return by_real[:rows] - by_imag[rows:], by_imag[:rows] + by_real[rows:]


def halves(value):
    high = value.astype(BF16)
    return high, (value - high.astype(F32)).astype(BF16)


def kernel(
    x_ref, o_ref,
    left, right, pairs, pair_low, chain, acc, end_left, end_right, end_sib,
    sibling, shifted, gathered, period, beside, turn, turn_sib, cross,
    late_shift, late_sib, late, final, tiles, landed,
    left_sem, right_sem, left_out, right_out, pair_sem, pair_out, first_sem, first_out, chain_sem, chain_out,
    ends_sem, ends_out, end_sib_sem, end_sib_out, sib_sem, sib_out, shift_sem, shift_out, gather_sem, gather_out,
    turn_sem, turn_out, late_sem, late_out, final_sem, final_out, relay_sem, all_sem, all_out,
):
    c = lax.axis_index("cuts")
    b = lax.axis_index("blk")
    xh = lax.div(b, 8)
    y = lax.rem(lax.div(b, 2), 4)
    h = lax.rem(b, 2)
    other = 1 - h
    sib = (c, b + 1 - 2 * h)
    opposite = (c, b + 8 - 16 * xh)

    def along_y(d):
        return (c, xh * 8 + lax.rem(y + d, 4) * 2 + h)

    def cut(k):
        return (lax.rem(c + k + 32, 32), b)

    def cut_over(k):
        return (lax.rem(c + k + 32, 32), opposite[1])

    @pl.when(h == 0)
    def _():
        pltpu.make_async_copy(x_ref.at[0, :, :, pl.ds(0, 256)], right, right_sem).start()

    @pl.when(h == 1)
    def _():
        for r in range(4):
            for q in range(2):
                pltpu.make_async_copy(
                    x_ref.at[0, :, pl.ds(128 * r, 128), pl.ds(256 * q, 256)],
                    left.at[q, :, pl.ds(128 * r, 128)],
                    left_sem.at[r, q],
                ).start()

    barrier = pltpu.get_barrier_semaphore()
    greet = [sib, opposite] + [along_y(d) for d in (1, 2, 3)]
    greet += [cut(1), cut_over(1), cut(2), cut_over(2), cut(-2)]
    for device in greet:
        pl.semaphore_signal(barrier, inc=1, device_id=device, device_id_type=MESH)
    pl.semaphore_wait(barrier, len(greet))

    def relay(n):
        for way in (-1, 1):
            pl.semaphore_signal(relay_sem.at[n], inc=1, device_id=cut(way * (2 << n)), device_id_type=MESH)

    relay(0)

    @pl.when(h == 0)
    def _():
        send(x_ref.at[0, :, :, pl.ds(256, 256)], right, right_out, right_sem, sib)

    @pl.when(h == 1)
    def _():
        for r in range(4):
            for q in range(2):
                send(
                    x_ref.at[0, :, pl.ds(128 * r, 128), pl.ds(256 * q, 256)],
                    left.at[q, :, pl.ds(128 * r, 128)],
                    left_out.at[r, q],
                    left_sem.at[r, q],
                    sib,
                )

    arrived(right, right_sem)

    def pass_pair(r, d):
        block = pairs.at[y, :, pl.ds(pl.multiple_of(128 * r, 128), 128)]
        send(block, block, pair_out.at[d - 1, r], pair_sem.at[d - 1, r], along_y(d))

    def pair_chunk(r, carry):
        rows = pl.ds(pl.multiple_of(128 * r, 128), 128)
        for q in range(2):
            arrived(left.at[q, :, rows], left_sem.at[r, q])
        x0 = left[0, :, rows, :].reshape(256, 256)
        x1 = left[1, :, rows, :].reshape(256, 256)
        by = [dot(x0, right[i, :256]) + dot(x1, right[i, 256:]) for i in range(2)]
        for i, part in enumerate(combine(*by)):
            high, low = halves(part)
            pairs[y, i, rows, :] = high
            pair_low[i, rows, :] = low

        @pl.when(y != 3)
        def _():
            pass_pair(r, 1 + 2 * lax.rem(r, 2))

        @pl.when(y == 3)
        def _():
            p = lax.div(r, 2)
            for n in range(2):
                chip = 2 * lax.rem(r, 2) + n
                part = pl.ds(pl.multiple_of(128 * r + 64 * n, 64), 64)

                @pl.when(chip != 3)
                def _():
                    for low, src in enumerate((pairs.at[3, :, part], pair_low.at[:, part])):
                        send(
                            src, chain.at[0, h, low, :, p],
                            first_out.at[chip, low, p], first_sem.at[low, p],
                            (c, xh * 8 + chip * 2 + h),
                        )

        return carry

    lax.fori_loop(0, 4, pair_chunk, 0)

    pl.semaphore_wait(relay_sem.at[0], 2)
    relay(1)

    for r in range(4):
        d = 1 if r % 2 == 0 else 3

        @pl.when(y != (0 if d == 1 else 2))
        def _():
            block = pairs.at[lax.rem(y + 4 - d, 4), :, pl.ds(128 * r, 128)]
            arrived(block, pair_sem.at[d - 1, r])
            send(block, block, pair_out.at[1, r], pair_sem.at[1, r], along_y(d))

        @pl.when(y != 3)
        def _():
            pass_pair(r, 4 - d)

    def wait_pair(j):
        for d, chunks in ((1, (1, 3)), (2, (0, 1, 2, 3)), (3, (0, 2))):
            @pl.when(lax.rem(y - j + 4, 4) == d)
            def _():
                for r in chunks:
                    arrived(pairs.at[j, :, pl.ds(128 * r, 128)], pair_sem.at[d - 1, r])

    def exchange_chain(s):
        send(chain.at[s, h], chain.at[s, h], chain_out.at[s], chain_sem.at[s], sib)

    pl.semaphore_wait(relay_sem.at[1], 2)
    relay(2)

    @pl.when(y == 3)
    def _():
        for p in range(2):
            rows = pl.ds(256 * p + 192, 64)
            chain[0, h, 0, :, p] = pairs[3, :, rows, :]
            chain[0, h, 1, :, p] = pair_low[:, rows, :]

    @pl.when(y != 3)
    def _():
        for low in range(2):
            for p in range(2):
                arrived(chain.at[0, h, low, :, p], first_sem.at[low, p])

    exchange_chain(0)
    ends = []
    for s in range(3):
        j = 2 - s
        wait_pair(j)
        arrived(chain.at[s, other], chain_sem.at[s])
        x0 = chain[s, 0].reshape(512, 256)
        x1 = chain[s, 1].reshape(512, 256)
        for i in range(2):
            t = dot(x0, pairs[j, i, :256]) + dot(x1, pairs[j, i, 256:])
            acc[i] = t[:256] + t[256:]

        @pl.when(y == j)
        def _():
            for i in range(2):
                acc[i] += dot(x0[:256], pair_low[i, :256]) + dot(x1[:256], pair_low[i, 256:])

        for i, part in enumerate(combine(acc[0], acc[1])):
            part = part.reshape(2, 64, 256)
            if s < 2:
                chain[s + 1, h, 0, i], chain[s + 1, h, 1, i] = halves(part)
            else:
                ends.append(part.astype(BF16))
        if s < 2:
            exchange_chain(s + 1)

    @pl.when(xh == 0)
    def _():
        for q in range(2):
            end_right[q] = jnp.concatenate([part[:, :, 128 * q : 128 * q + 128] for part in ends], axis=2)

    @pl.when(xh == 1)
    def _():
        for i in range(2):
            end_left[i] = ends[i]

    def spread(src, level):
        for d in (1, 3, 2):
            send(
                src, gathered.at[level, :, y],
                gather_out.at[level, d - 1], gather_sem.at[level, d - 1], along_y(d),
            )

    def spread_arrived(level):
        for d in (1, 2, 3):
            arrived(gathered.at[level, :, lax.rem(y - d + 4, 4)], gather_sem.at[level, d - 1])

    def quarter_product(x, level, p):
        return dot(x, gathered[level, p].reshape(256, 256))

    def quarter(t):
        rows = t.shape[0] // 2
        return t[:rows, :128] - t[rows:, 128:], t[:rows, 128:] + t[rows:, :128]

    def joined(blocks):
        rows = math.prod(blocks.shape[1:-1])
        return jnp.concatenate([blocks[0].reshape(rows, 128), blocks[1].reshape(rows, 128)], axis=1)

    def keep(t, level):
        parts = [part.reshape(2, 64, 128).astype(BF16) for part in quarter(t)]
        for i in range(2):
            period[level, i] = parts[i]
        side = jnp.concatenate(parts, axis=2)
        beside[level] = side
        gathered[level + 1, :, y] = side

    pl.semaphore_wait(relay_sem.at[2], 2)

    @pl.when(xh == 0)
    def _():
        send(end_right.at[1], end_right.at[0], ends_out, ends_sem, opposite)

    @pl.when(xh == 1)
    def _():
        send(end_left, end_left, ends_out, ends_sem, opposite)
        arrived(end_right.at[0], ends_sem)

    spread(end_right.at[0], 0)
    gathered[0, :, y] = end_right[0]

    @pl.when(xh == 0)
    def _():
        arrived(end_left, ends_sem)

    send(end_left, end_sib, end_sib_out, end_sib_sem, sib)
    spread_arrived(0)
    t = quarter_product(end_left[...].reshape(256, 256), 0, h)
    arrived(end_sib, end_sib_sem)
    keep(t + quarter_product(end_sib[...].reshape(256, 256), 0, other), 0)

    def double(level, k):
        for n, device in enumerate((cut(-k), cut_over(-k))):
            send(
                period.at[level], shifted.at[level, xh],
                shift_out.at[level, n], shift_sem.at[level, xh], device,
            )
        spread(beside.at[level], level + 1)
        for q in (xh, 1 - xh):
            arrived(shifted.at[level, q], shift_sem.at[level, q])
            send(
                shifted.at[level, q], sibling.at[level, q],
                sib_out.at[level, q], sib_sem.at[level, q], sib,
            )
        spread_arrived(level + 1)
        t = quarter_product(joined(shifted.at[level]), level + 1, h)
        for q in range(2):
            arrived(sibling.at[level, q], sib_sem.at[level, q])
        keep(t + quarter_product(joined(sibling.at[level]), level + 1, other), level + 1)
        return 2 * k

    lax.fori_loop(0, WIDE, double, jnp.int32(1))

    for half in range(2):
        send(
            period.at[WIDE, :, half], turn.at[xh], turn_out.at[half], turn_sem.at[xh],
            (lax.rem(c + 24, 32), half * 8 + y * 2 + h),
        )
    send(beside.at[WIDE], cross, late_out.at[0], late_sem.at[0], opposite)
    spread(beside.at[WIDE], WIDE + 1)
    arrived(cross, late_sem.at[0])
    spread(cross, WIDE + 2)
    gathered[WIDE + 2, :, y] = cross[...]
    for q in range(2):
        arrived(turn.at[q], turn_sem.at[q])
    send(turn, turn_sib, late_out.at[1], late_sem.at[1], sib)
    x0 = joined(turn)
    spread_arrived(WIDE + 1)
    own = quarter_product(x0, WIDE + 1, h)
    arrived(turn_sib, late_sem.at[1])
    x1 = joined(turn_sib)
    own = quarter(own + quarter_product(x1, WIDE + 1, other))
    spread_arrived(WIDE + 2)
    far = quarter(quarter_product(x0, WIDE + 2, h) + quarter_product(x1, WIDE + 2, other))
    for i in range(2):
        first = jnp.where(xh == 0, own[i], far[i])
        second = jnp.where(xh == 0, far[i], own[i])
        part = jnp.concatenate([first, second], axis=1).astype(BF16)
        late[0, i] = part
        final[i, xh, y] = part

    def spread_final(src, p, order):
        for d in (1, 3, 2):
            send(
                src, final.at[:, p, y],
                final_out.at[order, d - 1], final_sem.at[order, d - 1], along_y(d),
            )

    send(late.at[0], late_shift, late_out.at[2], late_sem.at[2], cut(-16))
    send(late.at[0], late.at[1], late_out.at[3], late_sem.at[3], opposite)
    spread_final(late.at[0], xh, 0)
    arrived(late.at[1], late_sem.at[3])
    spread_final(late.at[1], 1 - xh, 1)
    final[:, 1 - xh, y] = late[1]
    arrived(late_shift, late_sem.at[2])
    send(late_shift, late_sib, late_out.at[4], late_sem.at[4], sib)
    for order, p in enumerate((xh, 1 - xh)):
        for d in (1, 2, 3):
            arrived(final.at[:, p, lax.rem(y - d + 4, 4)], final_sem.at[order, d - 1])
    x0 = late_shift[...].reshape(128, 256)
    by = [dot(x0, final[i, h].reshape(256, 256)) for i in range(2)]
    arrived(late_sib, late_sem.at[4])
    x1 = late_sib[...].reshape(128, 256)
    by = [by[i] + dot(x1, final[i, other].reshape(256, 256)) for i in range(2)]
    real, imag = combine(*by)

    for core in range(2):
        re, im = (v[32 * core : 32 * core + 32] for v in (real, imag))
        turned = jnp.concatenate([re, im, im, -re], axis=0).T
        tiles[core] = turned.astype(BF16).reshape(16, 16, 128)
    same = lax.div(c, 16) == h

    def nearness(t):
        t = jnp.where(same, 15 - t, t)
        step = lax.div(t + 1, 2)
        return lax.rem(c + jnp.where(lax.rem(t, 2) == 1, step, 16 - step), 16)

    def scatter(t, carry):
        j = nearness(t)
        target = 16 * h + j
        for core in range(2):
            here = (target == c) & (h == core)

            @pl.when(here)
            def _():
                pltpu.make_async_copy(tiles.at[core, j], landed.at[c], all_sem).start()

            @pl.when(jnp.logical_not(here))
            def _():
                send(
                    tiles.at[core, j], landed.at[c], all_out.at[core, j], all_sem,
                    (target, xh * 8 + y * 2 + core),
                )
        return carry

    lax.fori_loop(0, 16, scatter, 0)

    @pl.when(h == 0)
    def _():
        arrived(right, right_out)

    @pl.when(h == 1)
    def _():
        for r in range(4):
            for q in range(2):
                arrived(left.at[q, :, pl.ds(128 * r, 128)], left_out.at[r, q])

    @pl.when(y != 3)
    def _():
        for d in (1, 3):
            for r in range(4):
                arrived(pairs.at[y, :, pl.ds(128 * r, 128)], pair_out.at[d - 1, r])

    @pl.when(y == 3)
    def _():
        for chip in range(3):
            for low in range(2):
                for p in range(2):
                    arrived(pair_low.at[:, pl.ds(0, 64)], first_out.at[chip, low, p])

    for r in range(4):
        @pl.when(y != (0 if r % 2 == 0 else 2))
        def _():
            arrived(pairs.at[y, :, pl.ds(128 * r, 128)], pair_out.at[1, r])

    for s in range(3):
        arrived(chain.at[s, h], chain_out.at[s])
    @pl.when(xh == 0)
    def _():
        arrived(end_right.at[1], ends_out)

    @pl.when(xh == 1)
    def _():
        arrived(end_left, ends_out)

    arrived(end_sib, end_sib_out)

    def level_sent(level, carry):
        for d in range(3):
            arrived(gathered.at[level, :, y], gather_out.at[level, d])
        return carry

    lax.fori_loop(0, WIDE + 3, level_sent, 0)

    def shift_sent(level, carry):
        for n in range(2):
            arrived(period.at[level], shift_out.at[level, n])
            arrived(sibling.at[level, n], sib_out.at[level, n])
        return carry

    lax.fori_loop(0, WIDE, shift_sent, 0)
    for half in range(2):
        arrived(turn.at[half], turn_out.at[half])
    for n in range(5):
        arrived(cross if n == 0 else late.at[0], late_out.at[n])
    for order in range(2):
        for d in range(3):
            arrived(late.at[0], final_out.at[order, d])

    def scatter_sent(j, carry):
        for core in range(2):
            @pl.when(jnp.logical_not((16 * h + j == c) & (h == core)))
            def _():
                arrived(tiles.at[core, j], all_out.at[core, j])
        return carry

    lax.fori_loop(0, 16, scatter_sent, 0)
    arrived(landed, all_sem)
    o_ref[...] = landed[...]


def sidebands(x_ref, o_ref):
    lane = lax.broadcasted_iota(jnp.int32, (16, 128), 1)
    sign = jnp.where(lane < 64, 1.0, -1.0).astype(F32)
    terms = [x_ref[int(format(n, "05b")[::-1], 2)].astype(F32) for n in range(32)]
    span = 1
    while span < 32:
        for start in range(0, 32, 2 * span):
            for n in range(start, start + span):
                angle = math.pi * (n - start) / span
                upper = terms[n + span]
                if n > start:
                    quarter_turn = pltpu.roll(upper, 64, 1) * sign
                    if 2 * (n - start) == span:
                        upper = quarter_turn
                    else:
                        upper = math.cos(angle) * upper + math.sin(angle) * quarter_turn
                terms[n], terms[n + span] = terms[n] + upper, terms[n] - upper
        span *= 2
    for n, term in enumerate(terms):
        term = term * math.sqrt(512 / 32)
        o_ref[n, 0] = term[:, :32]
        o_ref[n, 1] = term[:, 32:64]


def per_device(steps):
    dma = pltpu.SemaphoreType.DMA
    landed = pl.pallas_call(
        kernel,
        out_shape=jax.ShapeDtypeStruct((32, 16, 128), BF16),
        in_specs=[pl.BlockSpec(memory_space=pl.ANY)],
        out_specs=pl.BlockSpec(memory_space=pltpu.VMEM),
        scratch_shapes=[
            pltpu.VMEM((2, 2, 512, 256), BF16),
            pltpu.VMEM((2, 512, 256), BF16),
            pltpu.VMEM((4, 2, 512, 256), BF16),
            pltpu.VMEM((2, 512, 256), BF16),
            pltpu.VMEM((3, 2, 2, 2, 2, 64, 256), BF16),
            pltpu.VMEM((2, 256, 256), F32),
            pltpu.VMEM((2, 2, 64, 256), BF16),
            pltpu.VMEM((2, 2, 64, 256), BF16),
            pltpu.VMEM((2, 2, 64, 256), BF16),
            pltpu.VMEM((WIDE, 2, 2, 2, 64, 128), BF16),
            pltpu.VMEM((WIDE, 2, 2, 2, 64, 128), BF16),
            pltpu.VMEM((WIDE + 3, 2, 4, 64, 256), BF16),
            pltpu.VMEM((WIDE + 1, 2, 2, 64, 128), BF16),
            pltpu.VMEM((WIDE + 1, 2, 64, 256), BF16),
            pltpu.VMEM((2, 2, 64, 128), BF16),
            pltpu.VMEM((2, 2, 64, 128), BF16),
            pltpu.VMEM((2, 64, 256), BF16),
            pltpu.VMEM((2, 64, 256), BF16),
            pltpu.VMEM((2, 64, 256), BF16),
            pltpu.VMEM((2, 2, 64, 256), BF16),
            pltpu.VMEM((2, 2, 4, 64, 256), BF16),
            pltpu.VMEM((2, 16, 16, 128), BF16),
            pltpu.VMEM((32, 16, 128), BF16),
            dma((4, 2)), dma, dma((4, 2)), dma,
            dma((3, 4)), dma((3, 4)), dma((2, 2)), dma((3, 2, 2)), dma((3,)), dma((3,)),
            dma, dma, dma, dma, dma((WIDE, 2)), dma((WIDE, 2)),
            dma((WIDE, 2)), dma((WIDE, 2)), dma((WIDE + 3, 3)), dma((WIDE + 3, 3)),
            dma((2,)), dma((2,)), dma((5,)), dma((5,)), dma((2, 3)), dma((2, 3)),
            pltpu.SemaphoreType.REGULAR((3,)), dma, dma((2, 16)),
        ],
        compiler_params=pltpu.CompilerParams(
            collective_id=0, has_side_effects=True, vmem_limit_bytes=60 * 1024 * 1024
        ),
        cost_estimate=pl.CostEstimate(
            flops=8 * 512 * 512 * 512 * 3, bytes_accessed=4 * 1024 * 1024, transcendentals=0
        ),
        name="propagate",
    )(steps)
    result = pl.pallas_call(
        sidebands,
        out_shape=jax.ShapeDtypeStruct((32, 2, 16, 32), F32),
        in_specs=[pl.BlockSpec(memory_space=pltpu.VMEM)],
        out_specs=pl.BlockSpec(memory_space=pltpu.VMEM),
        compiler_params=pltpu.CompilerParams(vmem_limit_bytes=16 * 1024 * 1024),
        name="sidebands",
    )(landed)
    return result.transpose(0, 1, 3, 2)


def solution(mesh):
    return jax.shard_map(
        per_device,
        mesh=mesh,
        in_specs=(P(("cuts", "blk"), None, None, None),),
        out_specs=P(None, None, "blk", "cuts"),
        check_vma=False,
    )
```

```python
import math

import jax
import jax.numpy as jnp
from jax import lax
from jax.experimental import pallas as pl
from jax.experimental.pallas import tpu as pltpu
from jax.sharding import PartitionSpec as P

MESH = pl.DeviceIdType.MESH
F32 = jnp.float32
BF16 = jnp.bfloat16
LEVELS = 5
WIDE = 3


def dot(a, b):
    return jnp.dot(a, b, preferred_element_type=F32)


def arrived(ref, sem):
    pltpu.make_async_copy(ref, ref, sem).wait()


def send(src, dst, send_sem, recv_sem, device):
    pltpu.make_async_remote_copy(
        src_ref=src,
        dst_ref=dst,
        send_sem=send_sem,
        recv_sem=recv_sem,
        device_id=device,
        device_id_type=MESH,
    ).start()


def combine(by_real, by_imag):
    rows = by_real.shape[0] // 2
    return by_real[:rows] - by_imag[rows:], by_imag[:rows] + by_real[rows:]


def halves(value):
    high = value.astype(BF16)
    return high, (value - high.astype(F32)).astype(BF16)


def sidebands(x_ref, o_ref):
    lane = lax.broadcasted_iota(jnp.int32, (16, 128), 1)
    sign = jnp.where(lane < 64, 1.0, -1.0).astype(F32)
    terms = [x_ref[int(format(n, "05b")[::-1], 2)].astype(F32) for n in range(32)]
    span = 1
    while span < 32:
        for start in range(0, 32, 2 * span):
            for n in range(start, start + span):
                angle = math.pi * (n - start) / span
                upper = terms[n + span]
                if n > start:
                    quarter_turn = pltpu.roll(upper, 64, 1) * sign
                    if 2 * (n - start) == span:
                        upper = quarter_turn
                    else:
                        upper = math.cos(angle) * upper + math.sin(angle) * quarter_turn
                terms[n], terms[n + span] = terms[n] + upper, terms[n] - upper
        span *= 2
    for n, term in enumerate(terms):
        term = term * math.sqrt(512 / 32)
        o_ref[n, 0] = term[:, :32]
        o_ref[n, 1] = term[:, 32:64]


def kernel(
    x_ref, o_ref,
    left, right, pairs, pair_low, chain, acc, end_left, end_right, end_sib,
    sibling, shifted, gathered, period, beside, turn, turn_sib, cross,
    late_shift, late_sib, late, final, tiles, landed,
    left_sem, right_sem, left_out, right_out, pair_sem, pair_out, first_sem, first_out, chain_sem, chain_out,
    ends_sem, ends_out, end_sib_sem, end_sib_out, sib_sem, sib_out, shift_sem, shift_out, gather_sem, gather_out,
    turn_sem, turn_out, late_sem, late_out, final_sem, final_out, relay_sem, all_sem, all_out,
):
    c = lax.axis_index("cuts")
    b = lax.axis_index("blk")
    xh = lax.div(b, 8)
    y = lax.rem(lax.div(b, 2), 4)
    h = lax.rem(b, 2)
    other = 1 - h
    sib = (c, b + 1 - 2 * h)
    opposite = (c, b + 8 - 16 * xh)

    def along_y(d):
        return (c, xh * 8 + lax.rem(y + d, 4) * 2 + h)

    def cut(k):
        return (lax.rem(c + k + 32, 32), b)

    def cut_over(k):
        return (lax.rem(c + k + 32, 32), opposite[1])

    @pl.when(h == 0)
    def _():
        pltpu.make_async_copy(x_ref.at[0, :, :, pl.ds(0, 256)], right, right_sem).start()

    @pl.when(h == 1)
    def _():
        for r in range(4):
            for q in range(2):
                pltpu.make_async_copy(
                    x_ref.at[0, :, pl.ds(128 * r, 128), pl.ds(256 * q, 256)],
                    left.at[q, :, pl.ds(128 * r, 128)],
                    left_sem.at[r, q],
                ).start()

    barrier = pltpu.get_barrier_semaphore()
    greet = [sib, opposite] + [along_y(d) for d in (1, 2, 3)]
    greet += [cut(1), cut_over(1), cut(2), cut_over(2), cut(-2)]
    for device in greet:
        pl.semaphore_signal(barrier, inc=1, device_id=device, device_id_type=MESH)
    pl.semaphore_wait(barrier, len(greet))

    def relay(n):
        for way in (-1, 1):
            pl.semaphore_signal(relay_sem.at[n], inc=1, device_id=cut(way * (2 << n)), device_id_type=MESH)

    relay(0)

    @pl.when(h == 0)
    def _():
        send(x_ref.at[0, :, :, pl.ds(256, 256)], right, right_out, right_sem, sib)

    @pl.when(h == 1)
    def _():
        for r in range(4):
            for q in range(2):
                send(
                    x_ref.at[0, :, pl.ds(128 * r, 128), pl.ds(256 * q, 256)],
                    left.at[q, :, pl.ds(128 * r, 128)],
                    left_out.at[r, q],
                    left_sem.at[r, q],
                    sib,
                )

    arrived(right, right_sem)

    def pass_pair(r, d):
        block = pairs.at[y, :, pl.ds(pl.multiple_of(128 * r, 128), 128)]
        send(block, block, pair_out.at[d - 1, r], pair_sem.at[d - 1, r], along_y(d))

    def pair_chunk(r, carry):
        rows = pl.ds(pl.multiple_of(128 * r, 128), 128)
        for q in range(2):
            arrived(left.at[q, :, rows], left_sem.at[r, q])
        x0 = left[0, :, rows, :].reshape(256, 256)
        x1 = left[1, :, rows, :].reshape(256, 256)
        by = [dot(x0, right[i, :256]) + dot(x1, right[i, 256:]) for i in range(2)]
        for i, part in enumerate(combine(*by)):
            high, low = halves(part)
            pairs[y, i, rows, :] = high
            pair_low[i, rows, :] = low

        @pl.when(y != 3)
        def _():
            pass_pair(r, 1 + 2 * lax.rem(r, 2))

        @pl.when(y == 3)
        def _():
            p = lax.div(r, 2)
            for n in range(2):
                chip = 2 * lax.rem(r, 2) + n
                part = pl.ds(pl.multiple_of(128 * r + 64 * n, 64), 64)

                @pl.when(chip != 3)
                def _():
                    for low, src in enumerate((pairs.at[3, :, part], pair_low.at[:, part])):
                        send(
                            src, chain.at[0, h, low, :, p],
                            first_out.at[chip, low, p], first_sem.at[low, p],
                            (c, xh * 8 + chip * 2 + h),
                        )

        return carry

    lax.fori_loop(0, 4, pair_chunk, 0)

    pl.semaphore_wait(relay_sem.at[0], 2)
    relay(1)

    for r in range(4):
        d = 1 if r % 2 == 0 else 3

        @pl.when(y != (0 if d == 1 else 2))
        def _():
            block = pairs.at[lax.rem(y + 4 - d, 4), :, pl.ds(128 * r, 128)]
            arrived(block, pair_sem.at[d - 1, r])
            send(block, block, pair_out.at[1, r], pair_sem.at[1, r], along_y(d))

        @pl.when(y != 3)
        def _():
            pass_pair(r, 4 - d)

    def wait_pair(j):
        for d, chunks in ((1, (1, 3)), (2, (0, 1, 2, 3)), (3, (0, 2))):
            @pl.when(lax.rem(y - j + 4, 4) == d)
            def _():
                for r in chunks:
                    arrived(pairs.at[j, :, pl.ds(128 * r, 128)], pair_sem.at[d - 1, r])

    def exchange_chain(s):
        send(chain.at[s, h], chain.at[s, h], chain_out.at[s], chain_sem.at[s], sib)

    pl.semaphore_wait(relay_sem.at[1], 2)
    relay(2)

    @pl.when(y == 3)
    def _():
        for p in range(2):
            rows = pl.ds(256 * p + 192, 64)
            chain[0, h, 0, :, p] = pairs[3, :, rows, :]
            chain[0, h, 1, :, p] = pair_low[:, rows, :]

    @pl.when(y != 3)
    def _():
        for low in range(2):
            for p in range(2):
                arrived(chain.at[0, h, low, :, p], first_sem.at[low, p])

    exchange_chain(0)
    ends = []
    for s in range(3):
        j = 2 - s
        wait_pair(j)
        for q in (h, other):
            if q is other:
                arrived(chain.at[s, other], chain_sem.at[s])
            rows = pl.ds(pl.multiple_of(256 * q, 256), 256)
            x = chain[s, q].reshape(512, 256)
            for i in range(2):
                t = dot(x, pairs[j, i, rows, :])
                t = t[:256] + t[256:]
                if q is h:
                    acc[i] = t
                else:
                    acc[i] += t

            @pl.when(y == j)
            def _():
                for i in range(2):
                    acc[i] += dot(x[:256], pair_low[i, rows, :])

        for i, part in enumerate(combine(acc[0], acc[1])):
            part = part.reshape(2, 64, 256)
            if s < 2:
                chain[s + 1, h, 0, i], chain[s + 1, h, 1, i] = halves(part)
            else:
                ends.append(part.astype(BF16))
        if s < 2:
            exchange_chain(s + 1)

    @pl.when(xh == 0)
    def _():
        for q in range(2):
            end_right[q] = jnp.concatenate([part[:, :, 128 * q : 128 * q + 128] for part in ends], axis=2)

    @pl.when(xh == 1)
    def _():
        for i in range(2):
            end_left[i] = ends[i]

    def spread(src, level):
        for d in (1, 3, 2):
            send(
                src, gathered.at[level, :, y],
                gather_out.at[level, d - 1], gather_sem.at[level, d - 1], along_y(d),
            )

    def spread_arrived(level):
        for d in (1, 2, 3):
            arrived(gathered.at[level, :, lax.rem(y - d + 4, 4)], gather_sem.at[level, d - 1])

    def quarter_product(x, level, p):
        return dot(x, gathered[level, p].reshape(256, 256))

    def quarter(t):
        rows = t.shape[0] // 2
        return t[:rows, :128] - t[rows:, 128:], t[:rows, 128:] + t[rows:, :128]

    def joined(blocks):
        rows = math.prod(blocks.shape[1:-1])
        return jnp.concatenate([blocks[0].reshape(rows, 128), blocks[1].reshape(rows, 128)], axis=1)

    def keep(t, level):
        parts = [part.reshape(2, 64, 128).astype(BF16) for part in quarter(t)]
        for i in range(2):
            period[level, i] = parts[i]
        side = jnp.concatenate(parts, axis=2)
        beside[level] = side
        gathered[level + 1, :, y] = side

    pl.semaphore_wait(relay_sem.at[2], 2)

    @pl.when(xh == 0)
    def _():
        send(end_right.at[1], end_right.at[0], ends_out, ends_sem, opposite)

    @pl.when(xh == 1)
    def _():
        send(end_left, end_left, ends_out, ends_sem, opposite)
        arrived(end_right.at[0], ends_sem)

    spread(end_right.at[0], 0)
    gathered[0, :, y] = end_right[0]

    @pl.when(xh == 0)
    def _():
        arrived(end_left, ends_sem)

    send(end_left, end_sib, end_sib_out, end_sib_sem, sib)
    spread_arrived(0)
    t = quarter_product(end_left[...].reshape(256, 256), 0, h)
    arrived(end_sib, end_sib_sem)
    keep(t + quarter_product(end_sib[...].reshape(256, 256), 0, other), 0)

    def double(level, k):
        for n, device in enumerate((cut_over(-k), cut(-k))):
            send(
                period.at[level], shifted.at[level, xh],
                shift_out.at[level, n], shift_sem.at[level, xh], device,
            )
        spread(beside.at[level], level + 1)
        for q in (xh, 1 - xh):
            arrived(shifted.at[level, q], shift_sem.at[level, q])
            send(
                shifted.at[level, q], sibling.at[level, q],
                sib_out.at[level, q], sib_sem.at[level, q], sib,
            )
        spread_arrived(level + 1)
        t = quarter_product(joined(shifted.at[level]), level + 1, h)
        for q in range(2):
            arrived(sibling.at[level, q], sib_sem.at[level, q])
        keep(t + quarter_product(joined(sibling.at[level]), level + 1, other), level + 1)
        return 2 * k

    lax.fori_loop(0, WIDE, double, jnp.int32(1))

    send(beside.at[WIDE], cross, late_out.at[0], late_sem.at[0], opposite)
    for half in (1 - xh, xh):
        send(
            period.at[WIDE, :, half], turn.at[xh], turn_out.at[half], turn_sem.at[xh],
            (lax.rem(c + 24, 32), half * 8 + y * 2 + h),
        )
    spread(beside.at[WIDE], WIDE + 1)
    arrived(cross, late_sem.at[0])
    spread(cross, WIDE + 2)
    gathered[WIDE + 2, :, y] = cross[...]
    for q in range(2):
        arrived(turn.at[q], turn_sem.at[q])
    send(turn, turn_sib, late_out.at[1], late_sem.at[1], sib)
    x0 = joined(turn)
    spread_arrived(WIDE + 1)
    own = quarter_product(x0, WIDE + 1, h)
    arrived(turn_sib, late_sem.at[1])
    x1 = joined(turn_sib)
    own = quarter(own + quarter_product(x1, WIDE + 1, other))
    spread_arrived(WIDE + 2)
    far = quarter(quarter_product(x0, WIDE + 2, h) + quarter_product(x1, WIDE + 2, other))
    for i in range(2):
        first = jnp.where(xh == 0, own[i], far[i])
        second = jnp.where(xh == 0, far[i], own[i])
        part = jnp.concatenate([first, second], axis=1).astype(BF16)
        late[0, i] = part
        final[i, xh, y] = part

    def spread_final(src, p, order):
        for d in (1, 3, 2):
            send(
                src, final.at[:, p, y],
                final_out.at[order, d - 1], final_sem.at[order, d - 1], along_y(d),
            )

    send(late.at[0], late_shift, late_out.at[2], late_sem.at[2], cut(-16))
    send(late.at[0], late.at[1], late_out.at[3], late_sem.at[3], opposite)
    spread_final(late.at[0], xh, 0)
    arrived(late.at[1], late_sem.at[3])
    spread_final(late.at[1], 1 - xh, 1)
    final[:, 1 - xh, y] = late[1]
    arrived(late_shift, late_sem.at[2])
    send(late_shift, late_sib, late_out.at[4], late_sem.at[4], sib)
    for order, p in enumerate((xh, 1 - xh)):
        for d in (1, 2, 3):
            arrived(final.at[:, p, lax.rem(y - d + 4, 4)], final_sem.at[order, d - 1])
    x0 = late_shift[...].reshape(128, 256)
    by = [dot(x0, final[i, h].reshape(256, 256)) for i in range(2)]
    arrived(late_sib, late_sem.at[4])
    x1 = late_sib[...].reshape(128, 256)
    by = [by[i] + dot(x1, final[i, other].reshape(256, 256)) for i in range(2)]
    real, imag = combine(*by)

    for core in range(2):
        re, im = (v[32 * core : 32 * core + 32] for v in (real, imag))
        turned = jnp.concatenate([re, im, im, -re], axis=0).T
        tiles[core] = turned.astype(BF16).reshape(16, 16, 128)
    same = lax.div(c, 16) == h

    def nearness(t):
        t = jnp.where(same, 15 - t, t)
        step = lax.div(t + 1, 2)
        return lax.rem(c + jnp.where(lax.rem(t, 2) == 1, step, 16 - step), 16)

    def scatter(t, carry):
        j = nearness(t)
        target = 16 * h + j
        for core in range(2):
            here = (target == c) & (h == core)

            @pl.when(here)
            def _():
                pltpu.make_async_copy(tiles.at[core, j], landed.at[c], all_sem).start()

            @pl.when(jnp.logical_not(here))
            def _():
                send(
                    tiles.at[core, j], landed.at[c], all_out.at[core, j], all_sem,
                    (target, xh * 8 + y * 2 + core),
                )
        return carry

    lax.fori_loop(0, 16, scatter, 0)

    @pl.when(h == 0)
    def _():
        arrived(right, right_out)

    @pl.when(h == 1)
    def _():
        for r in range(4):
            for q in range(2):
                arrived(left.at[q, :, pl.ds(128 * r, 128)], left_out.at[r, q])

    @pl.when(y != 3)
    def _():
        for d in (1, 3):
            for r in range(4):
                arrived(pairs.at[y, :, pl.ds(128 * r, 128)], pair_out.at[d - 1, r])

    @pl.when(y == 3)
    def _():
        for chip in range(3):
            for low in range(2):
                for p in range(2):
                    arrived(pair_low.at[:, pl.ds(0, 64)], first_out.at[chip, low, p])

    for r in range(4):
        @pl.when(y != (0 if r % 2 == 0 else 2))
        def _():
            arrived(pairs.at[y, :, pl.ds(128 * r, 128)], pair_out.at[1, r])

    for s in range(3):
        arrived(chain.at[s, h], chain_out.at[s])
    @pl.when(xh == 0)
    def _():
        arrived(end_right.at[1], ends_out)

    @pl.when(xh == 1)
    def _():
        arrived(end_left, ends_out)

    arrived(end_sib, end_sib_out)

    def level_sent(level, carry):
        for d in range(3):
            arrived(gathered.at[level, :, y], gather_out.at[level, d])
        return carry

    lax.fori_loop(0, WIDE + 3, level_sent, 0)

    def shift_sent(level, carry):
        for n in range(2):
            arrived(period.at[level], shift_out.at[level, n])
            arrived(sibling.at[level, n], sib_out.at[level, n])
        return carry

    lax.fori_loop(0, WIDE, shift_sent, 0)
    for half in range(2):
        arrived(turn.at[half], turn_out.at[half])
    for n in range(5):
        arrived(cross if n == 0 else late.at[0], late_out.at[n])
    for order in range(2):
        for d in range(3):
            arrived(late.at[0], final_out.at[order, d])

    def scatter_sent(j, carry):
        for core in range(2):
            @pl.when(jnp.logical_not((16 * h + j == c) & (h == core)))
            def _():
                arrived(tiles.at[core, j], all_out.at[core, j])
        return carry

    lax.fori_loop(0, 16, scatter_sent, 0)
    arrived(landed, all_sem)
    sidebands(landed, o_ref)


def per_device(steps):
    dma = pltpu.SemaphoreType.DMA
    result = pl.pallas_call(
        kernel,
        out_shape=jax.ShapeDtypeStruct((32, 2, 16, 32), F32),
        in_specs=[pl.BlockSpec(memory_space=pl.ANY)],
        out_specs=pl.BlockSpec(memory_space=pltpu.VMEM),
        scratch_shapes=[
            pltpu.VMEM((2, 2, 512, 256), BF16),
            pltpu.VMEM((2, 512, 256), BF16),
            pltpu.VMEM((4, 2, 512, 256), BF16),
            pltpu.VMEM((2, 512, 256), BF16),
            pltpu.VMEM((3, 2, 2, 2, 2, 64, 256), BF16),
            pltpu.VMEM((2, 256, 256), F32),
            pltpu.VMEM((2, 2, 64, 256), BF16),
            pltpu.VMEM((2, 2, 64, 256), BF16),
            pltpu.VMEM((2, 2, 64, 256), BF16),
            pltpu.VMEM((WIDE, 2, 2, 2, 64, 128), BF16),
            pltpu.VMEM((WIDE, 2, 2, 2, 64, 128), BF16),
            pltpu.VMEM((WIDE + 3, 2, 4, 64, 256), BF16),
            pltpu.VMEM((WIDE + 1, 2, 2, 64, 128), BF16),
            pltpu.VMEM((WIDE + 1, 2, 64, 256), BF16),
            pltpu.VMEM((2, 2, 64, 128), BF16),
            pltpu.VMEM((2, 2, 64, 128), BF16),
            pltpu.VMEM((2, 64, 256), BF16),
            pltpu.VMEM((2, 64, 256), BF16),
            pltpu.VMEM((2, 64, 256), BF16),
            pltpu.VMEM((2, 2, 64, 256), BF16),
            pltpu.VMEM((2, 2, 4, 64, 256), BF16),
            pltpu.VMEM((2, 16, 16, 128), BF16),
            pltpu.VMEM((32, 16, 128), BF16),
            dma((4, 2)), dma, dma((4, 2)), dma,
            dma((3, 4)), dma((3, 4)), dma((2, 2)), dma((3, 2, 2)), dma((3,)), dma((3,)),
            dma, dma, dma, dma, dma((WIDE, 2)), dma((WIDE, 2)),
            dma((WIDE, 2)), dma((WIDE, 2)), dma((WIDE + 3, 3)), dma((WIDE + 3, 3)),
            dma((2,)), dma((2,)), dma((5,)), dma((5,)), dma((2, 3)), dma((2, 3)),
            pltpu.SemaphoreType.REGULAR((3,)), dma, dma((2, 16)),
        ],
        compiler_params=pltpu.CompilerParams(
            collective_id=0, has_side_effects=True, vmem_limit_bytes=60 * 1024 * 1024
        ),
        cost_estimate=pl.CostEstimate(
            flops=8 * 512 * 512 * 512 * 3, bytes_accessed=4 * 1024 * 1024, transcendentals=0
        ),
        name="propagate",
    )(steps)
    return result.transpose(0, 1, 3, 2)


def solution(mesh):
    return jax.shard_map(
        per_device,
        mesh=mesh,
        in_specs=(P(("cuts", "blk"), None, None, None),),
        out_specs=P(None, None, "blk", "cuts"),
        check_vma=False,
    )
```

```python
import math

import jax
import jax.numpy as jnp
from jax import lax
from jax.experimental import pallas as pl
from jax.experimental.pallas import tpu as pltpu
from jax.sharding import PartitionSpec as P

MESH = pl.DeviceIdType.MESH
F32 = jnp.float32
BF16 = jnp.bfloat16
LEVELS = 5
WIDE = 3


def dot(a, b):
    return jnp.dot(a, b, preferred_element_type=F32)


def arrived(ref, sem):
    pltpu.make_async_copy(ref, ref, sem).wait()


def send(src, dst, send_sem, recv_sem, device):
    pltpu.make_async_remote_copy(
        src_ref=src,
        dst_ref=dst,
        send_sem=send_sem,
        recv_sem=recv_sem,
        device_id=device,
        device_id_type=MESH,
    ).start()


def combine(by_real, by_imag):
    rows = by_real.shape[0] // 2
    return by_real[:rows] - by_imag[rows:], by_imag[:rows] + by_real[rows:]


def halves(value):
    high = value.astype(BF16)
    return high, (value - high.astype(F32)).astype(BF16)


def sidebands(x_ref, o_ref):
    lane = lax.broadcasted_iota(jnp.int32, (16, 128), 1)
    sign = jnp.where(lane < 64, 1.0, -1.0).astype(F32)
    terms = [x_ref[int(format(n, "05b")[::-1], 2)].astype(F32) for n in range(32)]
    span = 1
    while span < 32:
        for start in range(0, 32, 2 * span):
            for n in range(start, start + span):
                angle = math.pi * (n - start) / span
                upper = terms[n + span]
                if n > start:
                    quarter_turn = pltpu.roll(upper, 64, 1) * sign
                    if 2 * (n - start) == span:
                        upper = quarter_turn
                    else:
                        upper = math.cos(angle) * upper + math.sin(angle) * quarter_turn
                terms[n], terms[n + span] = terms[n] + upper, terms[n] - upper
        span *= 2
    for n, term in enumerate(terms):
        term = term * math.sqrt(512 / 32)
        o_ref[n, 0] = term[:, :32]
        o_ref[n, 1] = term[:, 32:64]


def kernel(
    x_ref, o_ref,
    left, right, pairs, pair_low, chain, acc, end_left, end_right, end_sib,
    sibling, shifted, gathered, period, beside, turn, turn_sib, cross,
    late_shift, late_sib, late, final, tiles, landed,
    left_sem, right_sem, left_out, right_out, pair_sem, pair_out, first_sem, first_out, chain_sem, chain_out,
    ends_sem, ends_out, end_sib_sem, end_sib_out, sib_sem, sib_out, shift_sem, shift_out, gather_sem, gather_out,
    turn_sem, turn_out, late_sem, late_out, final_sem, final_out, relay_sem, all_sem, all_out,
):
    c = lax.axis_index("cuts")
    b = lax.axis_index("blk")
    xh = lax.div(b, 8)
    y = lax.rem(lax.div(b, 2), 4)
    h = lax.rem(b, 2)
    other = 1 - h
    sib = (c, b + 1 - 2 * h)
    opposite = (c, b + 8 - 16 * xh)

    def along_y(d):
        return (c, xh * 8 + lax.rem(y + d, 4) * 2 + h)

    def cut(k):
        return (lax.rem(c + k + 32, 32), b)

    def cut_over(k):
        return (lax.rem(c + k + 32, 32), opposite[1])

    @pl.when(h == 0)
    def _():
        pltpu.make_async_copy(x_ref.at[0, :, :, pl.ds(0, 256)], right, right_sem).start()

    @pl.when(h == 1)
    def _():
        for r in range(4):
            for q in range(2):
                pltpu.make_async_copy(
                    x_ref.at[0, :, pl.ds(128 * r, 128), pl.ds(256 * q, 256)],
                    left.at[q, :, pl.ds(128 * r, 128)],
                    left_sem.at[r, q],
                ).start()

    barrier = pltpu.get_barrier_semaphore()
    greet = [sib, opposite] + [along_y(d) for d in (1, 2, 3)]
    greet += [cut(1), cut_over(1), cut(2), cut_over(2), cut(-2)]
    for device in greet:
        pl.semaphore_signal(barrier, inc=1, device_id=device, device_id_type=MESH)
    pl.semaphore_wait(barrier, len(greet))

    def relay(n):
        for way in (-1, 1):
            pl.semaphore_signal(relay_sem.at[n], inc=1, device_id=cut(way * (2 << n)), device_id_type=MESH)

    relay(0)

    @pl.when(h == 0)
    def _():
        send(x_ref.at[0, :, :, pl.ds(256, 256)], right, right_out, right_sem, sib)

    @pl.when(h == 1)
    def _():
        for r in range(4):
            for q in range(2):
                send(
                    x_ref.at[0, :, pl.ds(128 * r, 128), pl.ds(256 * q, 256)],
                    left.at[q, :, pl.ds(128 * r, 128)],
                    left_out.at[r, q],
                    left_sem.at[r, q],
                    sib,
                )

    arrived(right, right_sem)

    def pass_pair(r, d):
        block = pairs.at[y, :, pl.ds(pl.multiple_of(128 * r, 128), 128)]
        send(block, block, pair_out.at[d - 1, r], pair_sem.at[d - 1, r], along_y(d))

    def pair_chunk(r, carry):
        rows = pl.ds(pl.multiple_of(128 * r, 128), 128)
        for q in range(2):
            arrived(left.at[q, :, rows], left_sem.at[r, q])
        x0 = left[0, :, rows, :].reshape(256, 256)
        x1 = left[1, :, rows, :].reshape(256, 256)
        by = [dot(x0, right[i, :256]) + dot(x1, right[i, 256:]) for i in range(2)]
        for i, part in enumerate(combine(*by)):
            high, low = halves(part)
            pairs[y, i, rows, :] = high
            pair_low[i, rows, :] = low

        @pl.when(y != 3)
        def _():
            pass_pair(r, 1 + 2 * lax.rem(r, 2))

        @pl.when(y == 3)
        def _():
            p = lax.div(r, 2)
            for n in range(2):
                chip = 2 * lax.rem(r, 2) + n
                part = pl.ds(pl.multiple_of(128 * r + 64 * n, 64), 64)

                @pl.when(chip != 3)
                def _():
                    for low, src in enumerate((pairs.at[3, :, part], pair_low.at[:, part])):
                        send(
                            src, chain.at[0, h, low, :, p],
                            first_out.at[chip, low, p], first_sem.at[low, p],
                            (c, xh * 8 + chip * 2 + h),
                        )

        return carry

    lax.fori_loop(0, 4, pair_chunk, 0)

    pl.semaphore_wait(relay_sem.at[0], 2)
    relay(1)

    for r in range(4):
        d = 1 if r % 2 == 0 else 3

        @pl.when(y != (0 if d == 1 else 2))
        def _():
            block = pairs.at[lax.rem(y + 4 - d, 4), :, pl.ds(128 * r, 128)]
            arrived(block, pair_sem.at[d - 1, r])
            send(block, block, pair_out.at[1, r], pair_sem.at[1, r], along_y(d))

        @pl.when(y != 3)
        def _():
            pass_pair(r, 4 - d)

    def wait_pair(j):
        for d, chunks in ((1, (1, 3)), (2, (0, 1, 2, 3)), (3, (0, 2))):
            @pl.when(lax.rem(y - j + 4, 4) == d)
            def _():
                for r in chunks:
                    arrived(pairs.at[j, :, pl.ds(128 * r, 128)], pair_sem.at[d - 1, r])

    def exchange_chain(s):
        for low in range(2):
            part = chain.at[s, h, low]
            send(part, part, chain_out.at[s, low], chain_sem.at[s, low], sib)

    pl.semaphore_wait(relay_sem.at[1], 2)
    relay(2)

    @pl.when(y == 3)
    def _():
        for p in range(2):
            rows = pl.ds(256 * p + 192, 64)
            chain[0, h, 0, :, p] = pairs[3, :, rows, :]
            chain[0, h, 1, :, p] = pair_low[:, rows, :]

    @pl.when(y != 3)
    def _():
        for low in range(2):
            for p in range(2):
                arrived(chain.at[0, h, low, :, p], first_sem.at[low, p])

    exchange_chain(0)
    ends = []
    for s in range(3):
        j = 2 - s
        wait_pair(j)
        for q in (h, other):
            if q is other:
                for low in range(2):
                    arrived(chain.at[s, other, low], chain_sem.at[s, low])
            rows = pl.ds(pl.multiple_of(256 * q, 256), 256)
            x = chain[s, q].reshape(512, 256)
            for i in range(2):
                t = dot(x, pairs[j, i, rows, :])
                t = t[:256] + t[256:]
                if q is h:
                    acc[i] = t
                else:
                    acc[i] += t

            @pl.when(y == j)
            def _():
                for i in range(2):
                    acc[i] += dot(x[:256], pair_low[i, rows, :])

        for i, part in enumerate(combine(acc[0], acc[1])):
            part = part.reshape(2, 64, 256)
            if s < 2:
                chain[s + 1, h, 0, i], chain[s + 1, h, 1, i] = halves(part)
            else:
                ends.append(part.astype(BF16))
        if s < 2:
            exchange_chain(s + 1)

    @pl.when(xh == 0)
    def _():
        for q in range(2):
            end_right[q] = jnp.concatenate([part[:, :, 128 * q : 128 * q + 128] for part in ends], axis=2)

    @pl.when(xh == 1)
    def _():
        for i in range(2):
            end_left[i] = ends[i]

    def spread(src, level):
        for d in (1, 3, 2):
            send(
                src, gathered.at[level, :, y],
                gather_out.at[level, d - 1], gather_sem.at[level, d - 1], along_y(d),
            )

    def spread_arrived(level):
        for d in (1, 2, 3):
            arrived(gathered.at[level, :, lax.rem(y - d + 4, 4)], gather_sem.at[level, d - 1])

    def quarter_product(x, level, p):
        return dot(x, gathered[level, p].reshape(256, 256))

    def quarter(t):
        rows = t.shape[0] // 2
        return t[:rows, :128] - t[rows:, 128:], t[:rows, 128:] + t[rows:, :128]

    def joined(blocks):
        rows = math.prod(blocks.shape[1:-1])
        return jnp.concatenate([blocks[0].reshape(rows, 128), blocks[1].reshape(rows, 128)], axis=1)

    def keep(t, level):
        parts = [part.reshape(2, 64, 128).astype(BF16) for part in quarter(t)]
        for i in range(2):
            period[level, i] = parts[i]
        side = jnp.concatenate(parts, axis=2)
        beside[level] = side
        gathered[level + 1, :, y] = side

    pl.semaphore_wait(relay_sem.at[2], 2)

    @pl.when(xh == 0)
    def _():
        send(end_right.at[1], end_right.at[0], ends_out, ends_sem, opposite)

    @pl.when(xh == 1)
    def _():
        send(end_left, end_left, ends_out, ends_sem, opposite)
        arrived(end_right.at[0], ends_sem)

    spread(end_right.at[0], 0)
    gathered[0, :, y] = end_right[0]

    @pl.when(xh == 0)
    def _():
        arrived(end_left, ends_sem)

    send(end_left, end_sib, end_sib_out, end_sib_sem, sib)
    spread_arrived(0)
    t = quarter_product(end_left[...].reshape(256, 256), 0, h)
    arrived(end_sib, end_sib_sem)
    keep(t + quarter_product(end_sib[...].reshape(256, 256), 0, other), 0)

    def double(level, k):
        for n, device in enumerate((cut_over(-k), cut(-k))):
            send(
                period.at[level], shifted.at[level, xh],
                shift_out.at[level, n], shift_sem.at[level, xh], device,
            )
        spread(beside.at[level], level + 1)
        for q in (xh, 1 - xh):
            arrived(shifted.at[level, q], shift_sem.at[level, q])
            send(
                shifted.at[level, q], sibling.at[level, q],
                sib_out.at[level, q], sib_sem.at[level, q], sib,
            )
        spread_arrived(level + 1)
        t = quarter_product(joined(shifted.at[level]), level + 1, h)
        for q in range(2):
            arrived(sibling.at[level, q], sib_sem.at[level, q])
        keep(t + quarter_product(joined(sibling.at[level]), level + 1, other), level + 1)
        return 2 * k

    lax.fori_loop(0, WIDE, double, jnp.int32(1))

    send(beside.at[WIDE], cross, late_out.at[0], late_sem.at[0], opposite)
    for half in (1 - xh, xh):
        send(
            period.at[WIDE, :, half], turn.at[xh], turn_out.at[half], turn_sem.at[xh],
            (lax.rem(c + 24, 32), half * 8 + y * 2 + h),
        )
    spread(beside.at[WIDE], WIDE + 1)
    arrived(cross, late_sem.at[0])
    spread(cross, WIDE + 2)
    gathered[WIDE + 2, :, y] = cross[...]
    for q in range(2):
        arrived(turn.at[q], turn_sem.at[q])
    send(turn, turn_sib, late_out.at[1], late_sem.at[1], sib)
    x0 = joined(turn)
    spread_arrived(WIDE + 1)
    own = quarter_product(x0, WIDE + 1, h)
    arrived(turn_sib, late_sem.at[1])
    x1 = joined(turn_sib)
    own = quarter(own + quarter_product(x1, WIDE + 1, other))
    spread_arrived(WIDE + 2)
    far = quarter(quarter_product(x0, WIDE + 2, h) + quarter_product(x1, WIDE + 2, other))
    for i in range(2):
        first = jnp.where(xh == 0, own[i], far[i])
        second = jnp.where(xh == 0, far[i], own[i])
        part = jnp.concatenate([first, second], axis=1).astype(BF16)
        late[0, i] = part
        final[i, xh, y] = part

    def spread_final(src, p, order):
        for d in (1, 3, 2):
            send(
                src, final.at[:, p, y],
                final_out.at[order, d - 1], final_sem.at[order, d - 1], along_y(d),
            )

    send(late.at[0], late_shift, late_out.at[2], late_sem.at[2], cut(-16))
    send(late.at[0], late.at[1], late_out.at[3], late_sem.at[3], opposite)
    spread_final(late.at[0], xh, 0)
    arrived(late.at[1], late_sem.at[3])
    spread_final(late.at[1], 1 - xh, 1)
    final[:, 1 - xh, y] = late[1]
    arrived(late_shift, late_sem.at[2])
    send(late_shift, late_sib, late_out.at[4], late_sem.at[4], sib)
    for order, p in enumerate((xh, 1 - xh)):
        for d in (1, 2, 3):
            arrived(final.at[:, p, lax.rem(y - d + 4, 4)], final_sem.at[order, d - 1])
    x0 = late_shift[...].reshape(128, 256)
    by = [dot(x0, final[i, h].reshape(256, 256)) for i in range(2)]
    arrived(late_sib, late_sem.at[4])
    x1 = late_sib[...].reshape(128, 256)
    by = [by[i] + dot(x1, final[i, other].reshape(256, 256)) for i in range(2)]
    real, imag = combine(*by)

    for core in range(2):
        re, im = (v[32 * core : 32 * core + 32] for v in (real, imag))
        turned = jnp.concatenate([re, im, im, -re], axis=0).T
        tiles[core] = turned.astype(BF16).reshape(16, 16, 128)
    same = lax.div(c, 16) == h

    def nearness(t):
        t = jnp.where(same, 15 - t, t)
        step = lax.div(t + 1, 2)
        return lax.rem(c + jnp.where(lax.rem(t, 2) == 1, step, 16 - step), 16)

    def scatter(t, carry):
        j = nearness(t)
        target = 16 * h + j
        for core in range(2):
            here = (target == c) & (h == core)

            @pl.when(here)
            def _():
                pltpu.make_async_copy(tiles.at[core, j], landed.at[c], all_sem).start()

            @pl.when(jnp.logical_not(here))
            def _():
                send(
                    tiles.at[core, j], landed.at[c], all_out.at[core, j], all_sem,
                    (target, xh * 8 + y * 2 + core),
                )
        return carry

    lax.fori_loop(0, 16, scatter, 0)

    @pl.when(h == 0)
    def _():
        arrived(right, right_out)

    @pl.when(h == 1)
    def _():
        for r in range(4):
            for q in range(2):
                arrived(left.at[q, :, pl.ds(128 * r, 128)], left_out.at[r, q])

    @pl.when(y != 3)
    def _():
        for d in (1, 3):
            for r in range(4):
                arrived(pairs.at[y, :, pl.ds(128 * r, 128)], pair_out.at[d - 1, r])

    @pl.when(y == 3)
    def _():
        for chip in range(3):
            for low in range(2):
                for p in range(2):
                    arrived(pair_low.at[:, pl.ds(0, 64)], first_out.at[chip, low, p])

    for r in range(4):
        @pl.when(y != (0 if r % 2 == 0 else 2))
        def _():
            arrived(pairs.at[y, :, pl.ds(128 * r, 128)], pair_out.at[1, r])

    for s in range(3):
        for low in range(2):
            arrived(chain.at[s, h, low], chain_out.at[s, low])
    @pl.when(xh == 0)
    def _():
        arrived(end_right.at[1], ends_out)

    @pl.when(xh == 1)
    def _():
        arrived(end_left, ends_out)

    arrived(end_sib, end_sib_out)

    def level_sent(level, carry):
        for d in range(3):
            arrived(gathered.at[level, :, y], gather_out.at[level, d])
        return carry

    lax.fori_loop(0, WIDE + 3, level_sent, 0)

    def shift_sent(level, carry):
        for n in range(2):
            arrived(period.at[level], shift_out.at[level, n])
            arrived(sibling.at[level, n], sib_out.at[level, n])
        return carry

    lax.fori_loop(0, WIDE, shift_sent, 0)
    for half in range(2):
        arrived(turn.at[half], turn_out.at[half])
    for n in range(5):
        arrived(cross if n == 0 else late.at[0], late_out.at[n])
    for order in range(2):
        for d in range(3):
            arrived(late.at[0], final_out.at[order, d])

    def scatter_sent(j, carry):
        for core in range(2):
            @pl.when(jnp.logical_not((16 * h + j == c) & (h == core)))
            def _():
                arrived(tiles.at[core, j], all_out.at[core, j])
        return carry

    lax.fori_loop(0, 16, scatter_sent, 0)
    arrived(landed, all_sem)
    sidebands(landed, o_ref)


def per_device(steps):
    dma = pltpu.SemaphoreType.DMA
    result = pl.pallas_call(
        kernel,
        out_shape=jax.ShapeDtypeStruct((32, 2, 16, 32), F32),
        in_specs=[pl.BlockSpec(memory_space=pl.ANY)],
        out_specs=pl.BlockSpec(memory_space=pltpu.VMEM),
        scratch_shapes=[
            pltpu.VMEM((2, 2, 512, 256), BF16),
            pltpu.VMEM((2, 512, 256), BF16),
            pltpu.VMEM((4, 2, 512, 256), BF16),
            pltpu.VMEM((2, 512, 256), BF16),
            pltpu.VMEM((3, 2, 2, 2, 2, 64, 256), BF16),
            pltpu.VMEM((2, 256, 256), F32),
            pltpu.VMEM((2, 2, 64, 256), BF16),
            pltpu.VMEM((2, 2, 64, 256), BF16),
            pltpu.VMEM((2, 2, 64, 256), BF16),
            pltpu.VMEM((WIDE, 2, 2, 2, 64, 128), BF16),
            pltpu.VMEM((WIDE, 2, 2, 2, 64, 128), BF16),
            pltpu.VMEM((WIDE + 3, 2, 4, 64, 256), BF16),
            pltpu.VMEM((WIDE + 1, 2, 2, 64, 128), BF16),
            pltpu.VMEM((WIDE + 1, 2, 64, 256), BF16),
            pltpu.VMEM((2, 2, 64, 128), BF16),
            pltpu.VMEM((2, 2, 64, 128), BF16),
            pltpu.VMEM((2, 64, 256), BF16),
            pltpu.VMEM((2, 64, 256), BF16),
            pltpu.VMEM((2, 64, 256), BF16),
            pltpu.VMEM((2, 2, 64, 256), BF16),
            pltpu.VMEM((2, 2, 4, 64, 256), BF16),
            pltpu.VMEM((2, 16, 16, 128), BF16),
            pltpu.VMEM((32, 16, 128), BF16),
            dma((4, 2)), dma, dma((4, 2)), dma,
            dma((3, 4)), dma((3, 4)), dma((2, 2)), dma((3, 2, 2)), dma((3, 2)), dma((3, 2)),
            dma, dma, dma, dma, dma((WIDE, 2)), dma((WIDE, 2)),
            dma((WIDE, 2)), dma((WIDE, 2)), dma((WIDE + 3, 3)), dma((WIDE + 3, 3)),
            dma((2,)), dma((2,)), dma((5,)), dma((5,)), dma((2, 3)), dma((2, 3)),
            pltpu.SemaphoreType.REGULAR((3,)), dma, dma((2, 16)),
        ],
        compiler_params=pltpu.CompilerParams(
            collective_id=0, has_side_effects=True, vmem_limit_bytes=60 * 1024 * 1024
        ),
        cost_estimate=pl.CostEstimate(
            flops=8 * 512 * 512 * 512 * 3, bytes_accessed=4 * 1024 * 1024, transcendentals=0
        ),
        name="propagate",
    )(steps)
    return result.transpose(0, 1, 3, 2)


def solution(mesh):
    return jax.shard_map(
        per_device,
        mesh=mesh,
        in_specs=(P(("cuts", "blk"), None, None, None),),
        out_specs=P(None, None, "blk", "cuts"),
        check_vma=False,
    )
```

```python
import math

import jax
import jax.numpy as jnp
from jax import lax
from jax.experimental import pallas as pl
from jax.experimental.pallas import tpu as pltpu
from jax.sharding import PartitionSpec as P

MESH = pl.DeviceIdType.MESH
F32 = jnp.float32
BF16 = jnp.bfloat16
LEVELS = 5
WIDE = 3


def dot(a, b):
    return jnp.dot(a, b, preferred_element_type=F32)


def arrived(ref, sem):
    pltpu.make_async_copy(ref, ref, sem).wait()


def send(src, dst, send_sem, recv_sem, device):
    pltpu.make_async_remote_copy(
        src_ref=src,
        dst_ref=dst,
        send_sem=send_sem,
        recv_sem=recv_sem,
        device_id=device,
        device_id_type=MESH,
    ).start()


def combine(by_real, by_imag):
    rows = by_real.shape[0] // 2
    return by_real[:rows] - by_imag[rows:], by_imag[:rows] + by_real[rows:]


def halves(value):
    high = value.astype(BF16)
    return high, (value - high.astype(F32)).astype(BF16)


def sidebands(x_ref, o_ref):
    lane = lax.broadcasted_iota(jnp.int32, (16, 128), 1)
    sign = jnp.where(lane < 64, 1.0, -1.0).astype(F32)
    terms = [x_ref[int(format(n, "05b")[::-1], 2)].astype(F32) for n in range(32)]
    span = 1
    while span < 32:
        for start in range(0, 32, 2 * span):
            for n in range(start, start + span):
                angle = math.pi * (n - start) / span
                upper = terms[n + span]
                if n > start:
                    quarter_turn = pltpu.roll(upper, 64, 1) * sign
                    if 2 * (n - start) == span:
                        upper = quarter_turn
                    else:
                        upper = math.cos(angle) * upper + math.sin(angle) * quarter_turn
                terms[n], terms[n + span] = terms[n] + upper, terms[n] - upper
        span *= 2
    for n, term in enumerate(terms):
        term = term * math.sqrt(512 / 32)
        o_ref[n, 0] = term[:, :32]
        o_ref[n, 1] = term[:, 32:64]


def kernel(
    x_ref, o_ref,
    left, right, pairs, pair_low, chain, acc, end_left, end_right, end_sib,
    sibling, shifted, gathered, period, beside, turn, turn_sib, cross,
    late_shift, late_sib, late, final, tiles, landed,
    left_sem, right_sem, left_out, right_out, pair_sem, pair_out, first_sem, first_out, chain_sem, chain_out,
    ends_sem, ends_out, end_sib_sem, end_sib_out, sib_sem, sib_out, shift_sem, shift_out, gather_sem, gather_out,
    turn_sem, turn_out, late_sem, late_out, final_sem, final_out, relay_sem, all_sem, all_out,
):
    c = lax.axis_index("cuts")
    b = lax.axis_index("blk")
    xh = lax.div(b, 8)
    y = lax.rem(lax.div(b, 2), 4)
    h = lax.rem(b, 2)
    other = 1 - h
    sib = (c, b + 1 - 2 * h)
    opposite = (c, b + 8 - 16 * xh)

    def along_y(d):
        return (c, xh * 8 + lax.rem(y + d, 4) * 2 + h)

    def cut(k):
        return (lax.rem(c + k + 32, 32), b)

    def cut_over(k):
        return (lax.rem(c + k + 32, 32), opposite[1])

    @pl.when(h == 0)
    def _():
        pltpu.make_async_copy(x_ref.at[0, :, :, pl.ds(0, 256)], right, right_sem).start()

    @pl.when(h == 1)
    def _():
        for r in range(4):
            for q in range(2):
                pltpu.make_async_copy(
                    x_ref.at[0, :, pl.ds(128 * r, 128), pl.ds(256 * q, 256)],
                    left.at[q, :, pl.ds(128 * r, 128)],
                    left_sem.at[r, q],
                ).start()

    barrier = pltpu.get_barrier_semaphore()
    greet = [sib, opposite] + [along_y(d) for d in (1, 2, 3)]
    greet += [cut(1), cut_over(1), cut(2), cut_over(2), cut(-2)]
    for device in greet:
        pl.semaphore_signal(barrier, inc=1, device_id=device, device_id_type=MESH)
    pl.semaphore_wait(barrier, len(greet))

    def relay(n):
        for way in (-1, 1):
            pl.semaphore_signal(relay_sem.at[n], inc=1, device_id=cut(way * (2 << n)), device_id_type=MESH)

    relay(0)

    @pl.when(h == 0)
    def _():
        send(x_ref.at[0, :, :, pl.ds(256, 256)], right, right_out, right_sem, sib)

    @pl.when(h == 1)
    def _():
        for r in range(4):
            for q in range(2):
                send(
                    x_ref.at[0, :, pl.ds(128 * r, 128), pl.ds(256 * q, 256)],
                    left.at[q, :, pl.ds(128 * r, 128)],
                    left_out.at[r, q],
                    left_sem.at[r, q],
                    sib,
                )

    arrived(right, right_sem)

    def pass_pair(r, d):
        block = pairs.at[y, :, pl.ds(pl.multiple_of(128 * r, 128), 128)]
        send(block, block, pair_out.at[d - 1, r], pair_sem.at[d - 1, r], along_y(d))

    def pair_chunk(r, carry):
        rows = pl.ds(pl.multiple_of(128 * r, 128), 128)
        for q in range(2):
            arrived(left.at[q, :, rows], left_sem.at[r, q])
        x0 = left[0, :, rows, :].reshape(256, 256)
        x1 = left[1, :, rows, :].reshape(256, 256)
        by = [dot(x0, right[i, :256]) + dot(x1, right[i, 256:]) for i in range(2)]
        for i, part in enumerate(combine(*by)):
            high, low = halves(part)
            pairs[y, i, rows, :] = high
            pair_low[i, rows, :] = low

        @pl.when(y != 3)
        def _():
            pass_pair(r, 1 + 2 * lax.rem(r, 2))

        @pl.when(y == 3)
        def _():
            p = lax.div(r, 2)
            for n in range(2):
                chip = 2 * lax.rem(r, 2) + n
                part = pl.ds(pl.multiple_of(128 * r + 64 * n, 64), 64)

                @pl.when(chip != 3)
                def _():
                    for low, src in enumerate((pairs.at[3, :, part], pair_low.at[:, part])):
                        send(
                            src, chain.at[0, h, low, :, p],
                            first_out.at[chip, low, p], first_sem.at[low, p],
                            (c, xh * 8 + chip * 2 + h),
                        )

        return carry

    lax.fori_loop(0, 4, pair_chunk, 0)

    pl.semaphore_wait(relay_sem.at[0], 2)
    relay(1)

    for r in range(4):
        d = 1 if r % 2 == 0 else 3

        @pl.when(y != (0 if d == 1 else 2))
        def _():
            block = pairs.at[lax.rem(y + 4 - d, 4), :, pl.ds(128 * r, 128)]
            arrived(block, pair_sem.at[d - 1, r])
            send(block, block, pair_out.at[1, r], pair_sem.at[1, r], along_y(d))

        @pl.when(y != 3)
        def _():
            pass_pair(r, 4 - d)

    def wait_pair(j):
        for d, chunks in ((1, (1, 3)), (2, (0, 1, 2, 3)), (3, (0, 2))):
            @pl.when(lax.rem(y - j + 4, 4) == d)
            def _():
                for r in chunks:
                    arrived(pairs.at[j, :, pl.ds(128 * r, 128)], pair_sem.at[d - 1, r])

    def exchange_chain(s):
        send(chain.at[s, h], chain.at[s, h], chain_out.at[s], chain_sem.at[s], sib)

    pl.semaphore_wait(relay_sem.at[1], 2)
    relay(2)

    @pl.when(y == 3)
    def _():
        for p in range(2):
            rows = pl.ds(256 * p + 192, 64)
            chain[0, h, 0, :, p] = pairs[3, :, rows, :]
            chain[0, h, 1, :, p] = pair_low[:, rows, :]

    @pl.when(y != 3)
    def _():
        for low in range(2):
            for p in range(2):
                arrived(chain.at[0, h, low, :, p], first_sem.at[low, p])

    exchange_chain(0)
    ends = []
    for s in range(3):
        j = 2 - s
        wait_pair(j)
        for q in (h, other):
            if q is other:
                arrived(chain.at[s, other], chain_sem.at[s])
            rows = pl.ds(pl.multiple_of(256 * q, 256), 256)
            x = chain[s, q].reshape(512, 256)
            for i in range(2):
                t = dot(x, pairs[j, i, rows, :])
                t = t[:256] + t[256:]
                if q is h:
                    acc[i] = t
                else:
                    acc[i] += t

            @pl.when(y == j)
            def _():
                for i in range(2):
                    acc[i] += dot(x[:256], pair_low[i, rows, :])

        for i, part in enumerate(combine(acc[0], acc[1])):
            part = part.reshape(2, 64, 256)
            if s < 2:
                chain[s + 1, h, 0, i], chain[s + 1, h, 1, i] = halves(part)
            else:
                ends.append(part.astype(BF16))
        if s < 2:
            exchange_chain(s + 1)

    @pl.when(xh == 0)
    def _():
        for q in range(2):
            end_right[q] = jnp.concatenate([part[:, :, 128 * q : 128 * q + 128] for part in ends], axis=2)

    @pl.when(xh == 1)
    def _():
        for i in range(2):
            end_left[i] = ends[i]

    def spread(src, level):
        for d in (1, 3, 2):
            send(
                src, gathered.at[level, :, y],
                gather_out.at[level, d - 1], gather_sem.at[level, d - 1], along_y(d),
            )

    def spread_arrived(level):
        for d in (1, 2, 3):
            arrived(gathered.at[level, :, lax.rem(y - d + 4, 4)], gather_sem.at[level, d - 1])

    def quarter_product(x, level, p):
        return dot(x, gathered[level, p].reshape(256, 256))

    def quarter(t):
        rows = t.shape[0] // 2
        return t[:rows, :128] - t[rows:, 128:], t[:rows, 128:] + t[rows:, :128]

    def joined(blocks):
        rows = math.prod(blocks.shape[1:-1])
        return jnp.concatenate([blocks[0].reshape(rows, 128), blocks[1].reshape(rows, 128)], axis=1)

    def keep(t, level):
        parts = [part.reshape(2, 64, 128).astype(BF16) for part in quarter(t)]
        for i in range(2):
            period[level, i] = parts[i]
        side = jnp.concatenate(parts, axis=2)
        beside[level] = side
        gathered[level + 1, :, y] = side

    pl.semaphore_wait(relay_sem.at[2], 2)

    @pl.when(xh == 0)
    def _():
        send(end_right.at[1], end_right.at[0], ends_out, ends_sem, opposite)

    @pl.when(xh == 1)
    def _():
        send(end_left, end_left, ends_out, ends_sem, opposite)
        arrived(end_right.at[0], ends_sem)

    spread(end_right.at[0], 0)
    gathered[0, :, y] = end_right[0]

    @pl.when(xh == 0)
    def _():
        arrived(end_left, ends_sem)

    send(end_left, end_sib, end_sib_out, end_sib_sem, sib)
    spread_arrived(0)
    t = quarter_product(end_left[...].reshape(256, 256), 0, h)
    arrived(end_sib, end_sib_sem)
    keep(t + quarter_product(end_sib[...].reshape(256, 256), 0, other), 0)

    def double(level, k):
        for n, device in enumerate((cut_over(-k), cut(-k))):
            send(
                period.at[level], shifted.at[level, xh],
                shift_out.at[level, n], shift_sem.at[level, xh], device,
            )
        spread(beside.at[level], level + 1)
        for q in (xh, 1 - xh):
            arrived(shifted.at[level, q], shift_sem.at[level, q])
            send(
                shifted.at[level, q], sibling.at[level, q],
                sib_out.at[level, q], sib_sem.at[level, q], sib,
            )
        spread_arrived(level + 1)
        t = quarter_product(joined(shifted.at[level]), level + 1, h)
        for q in range(2):
            arrived(sibling.at[level, q], sib_sem.at[level, q])
        keep(t + quarter_product(joined(sibling.at[level]), level + 1, other), level + 1)
        return 2 * k

    lax.fori_loop(0, WIDE, double, jnp.int32(1))

    send(beside.at[WIDE], cross, late_out.at[0], late_sem.at[0], opposite)
    for half in (1 - xh, xh):
        send(
            period.at[WIDE, :, half], turn.at[xh], turn_out.at[half], turn_sem.at[xh],
            (lax.rem(c + 24, 32), half * 8 + y * 2 + h),
        )
    spread(beside.at[WIDE], WIDE + 1)
    arrived(cross, late_sem.at[0])
    spread(cross, WIDE + 2)
    gathered[WIDE + 2, :, y] = cross[...]
    for q in range(2):
        arrived(turn.at[q], turn_sem.at[q])
    send(turn, turn_sib, late_out.at[1], late_sem.at[1], sib)
    x0 = joined(turn)
    spread_arrived(WIDE + 1)
    own = quarter_product(x0, WIDE + 1, h)
    arrived(turn_sib, late_sem.at[1])
    x1 = joined(turn_sib)
    own = quarter(own + quarter_product(x1, WIDE + 1, other))
    spread_arrived(WIDE + 2)
    far = quarter(quarter_product(x0, WIDE + 2, h) + quarter_product(x1, WIDE + 2, other))
    for i in range(2):
        first = jnp.where(xh == 0, own[i], far[i])
        second = jnp.where(xh == 0, far[i], own[i])
        part = jnp.concatenate([first, second], axis=1).astype(BF16)
        late[0, i] = part
        final[i, xh, y] = part

    def spread_final(src, p, order):
        for d in (1, 3, 2):
            send(
                src, final.at[:, p, y],
                final_out.at[order, d - 1], final_sem.at[order, d - 1], along_y(d),
            )

    send(late.at[0], late.at[1], late_out.at[3], late_sem.at[3], opposite)
    send(late.at[0], late_shift, late_out.at[2], late_sem.at[2], cut(-16))
    spread_final(late.at[0], xh, 0)
    arrived(late.at[1], late_sem.at[3])
    spread_final(late.at[1], 1 - xh, 1)
    final[:, 1 - xh, y] = late[1]
    arrived(late_shift, late_sem.at[2])
    send(late_shift, late_sib, late_out.at[4], late_sem.at[4], sib)
    for order, p in enumerate((xh, 1 - xh)):
        for d in (1, 2, 3):
            arrived(final.at[:, p, lax.rem(y - d + 4, 4)], final_sem.at[order, d - 1])
    x0 = late_shift[...].reshape(128, 256)
    by = [dot(x0, final[i, h].reshape(256, 256)) for i in range(2)]
    arrived(late_sib, late_sem.at[4])
    x1 = late_sib[...].reshape(128, 256)
    by = [by[i] + dot(x1, final[i, other].reshape(256, 256)) for i in range(2)]
    real, imag = combine(*by)

    for core in range(2):
        re, im = (v[32 * core : 32 * core + 32] for v in (real, imag))
        turned = jnp.concatenate([re, im, im, -re], axis=0).T
        tiles[core] = turned.astype(BF16).reshape(16, 16, 128)
    same = lax.div(c, 16) == h

    def nearness(t):
        t = jnp.where(same, 15 - t, t)
        step = lax.div(t + 1, 2)
        return lax.rem(c + jnp.where(lax.rem(t, 2) == 1, step, 16 - step), 16)

    def scatter(t, carry):
        j = nearness(t)
        target = 16 * h + j
        for core in range(2):
            here = (target == c) & (h == core)

            @pl.when(here)
            def _():
                pltpu.make_async_copy(tiles.at[core, j], landed.at[c], all_sem).start()

            @pl.when(jnp.logical_not(here))
            def _():
                send(
                    tiles.at[core, j], landed.at[c], all_out.at[core, j], all_sem,
                    (target, xh * 8 + y * 2 + core),
                )
        return carry

    lax.fori_loop(0, 16, scatter, 0)

    @pl.when(h == 0)
    def _():
        arrived(right, right_out)

    @pl.when(h == 1)
    def _():
        for r in range(4):
            for q in range(2):
                arrived(left.at[q, :, pl.ds(128 * r, 128)], left_out.at[r, q])

    @pl.when(y != 3)
    def _():
        for d in (1, 3):
            for r in range(4):
                arrived(pairs.at[y, :, pl.ds(128 * r, 128)], pair_out.at[d - 1, r])

    @pl.when(y == 3)
    def _():
        for chip in range(3):
            for low in range(2):
                for p in range(2):
                    arrived(pair_low.at[:, pl.ds(0, 64)], first_out.at[chip, low, p])

    for r in range(4):
        @pl.when(y != (0 if r % 2 == 0 else 2))
        def _():
            arrived(pairs.at[y, :, pl.ds(128 * r, 128)], pair_out.at[1, r])

    for s in range(3):
        arrived(chain.at[s, h], chain_out.at[s])
    @pl.when(xh == 0)
    def _():
        arrived(end_right.at[1], ends_out)

    @pl.when(xh == 1)
    def _():
        arrived(end_left, ends_out)

    arrived(end_sib, end_sib_out)

    def level_sent(level, carry):
        for d in range(3):
            arrived(gathered.at[level, :, y], gather_out.at[level, d])
        return carry

    lax.fori_loop(0, WIDE + 3, level_sent, 0)

    def shift_sent(level, carry):
        for n in range(2):
            arrived(period.at[level], shift_out.at[level, n])
            arrived(sibling.at[level, n], sib_out.at[level, n])
        return carry

    lax.fori_loop(0, WIDE, shift_sent, 0)
    for half in range(2):
        arrived(turn.at[half], turn_out.at[half])
    for n in range(5):
        arrived(cross if n == 0 else late.at[0], late_out.at[n])
    for order in range(2):
        for d in range(3):
            arrived(late.at[0], final_out.at[order, d])

    def scatter_sent(j, carry):
        for core in range(2):
            @pl.when(jnp.logical_not((16 * h + j == c) & (h == core)))
            def _():
                arrived(tiles.at[core, j], all_out.at[core, j])
        return carry

    lax.fori_loop(0, 16, scatter_sent, 0)
    arrived(landed, all_sem)
    sidebands(landed, o_ref)


def per_device(steps):
    dma = pltpu.SemaphoreType.DMA
    result = pl.pallas_call(
        kernel,
        out_shape=jax.ShapeDtypeStruct((32, 2, 16, 32), F32),
        in_specs=[pl.BlockSpec(memory_space=pl.ANY)],
        out_specs=pl.BlockSpec(memory_space=pltpu.VMEM),
        scratch_shapes=[
            pltpu.VMEM((2, 2, 512, 256), BF16),
            pltpu.VMEM((2, 512, 256), BF16),
            pltpu.VMEM((4, 2, 512, 256), BF16),
            pltpu.VMEM((2, 512, 256), BF16),
            pltpu.VMEM((3, 2, 2, 2, 2, 64, 256), BF16),
            pltpu.VMEM((2, 256, 256), F32),
            pltpu.VMEM((2, 2, 64, 256), BF16),
            pltpu.VMEM((2, 2, 64, 256), BF16),
            pltpu.VMEM((2, 2, 64, 256), BF16),
            pltpu.VMEM((WIDE, 2, 2, 2, 64, 128), BF16),
            pltpu.VMEM((WIDE, 2, 2, 2, 64, 128), BF16),
            pltpu.VMEM((WIDE + 3, 2, 4, 64, 256), BF16),
            pltpu.VMEM((WIDE + 1, 2, 2, 64, 128), BF16),
            pltpu.VMEM((WIDE + 1, 2, 64, 256), BF16),
            pltpu.VMEM((2, 2, 64, 128), BF16),
            pltpu.VMEM((2, 2, 64, 128), BF16),
            pltpu.VMEM((2, 64, 256), BF16),
            pltpu.VMEM((2, 64, 256), BF16),
            pltpu.VMEM((2, 64, 256), BF16),
            pltpu.VMEM((2, 2, 64, 256), BF16),
            pltpu.VMEM((2, 2, 4, 64, 256), BF16),
            pltpu.VMEM((2, 16, 16, 128), BF16),
            pltpu.VMEM((32, 16, 128), BF16),
            dma((4, 2)), dma, dma((4, 2)), dma,
            dma((3, 4)), dma((3, 4)), dma((2, 2)), dma((3, 2, 2)), dma((3,)), dma((3,)),
            dma, dma, dma, dma, dma((WIDE, 2)), dma((WIDE, 2)),
            dma((WIDE, 2)), dma((WIDE, 2)), dma((WIDE + 3, 3)), dma((WIDE + 3, 3)),
            dma((2,)), dma((2,)), dma((5,)), dma((5,)), dma((2, 3)), dma((2, 3)),
            pltpu.SemaphoreType.REGULAR((3,)), dma, dma((2, 16)),
        ],
        compiler_params=pltpu.CompilerParams(
            collective_id=0, has_side_effects=True, vmem_limit_bytes=60 * 1024 * 1024
        ),
        cost_estimate=pl.CostEstimate(
            flops=8 * 512 * 512 * 512 * 3, bytes_accessed=4 * 1024 * 1024, transcendentals=0
        ),
        name="propagate",
    )(steps)
    return result.transpose(0, 1, 3, 2)


def solution(mesh):
    return jax.shard_map(
        per_device,
        mesh=mesh,
        in_specs=(P(("cuts", "blk"), None, None, None),),
        out_specs=P(None, None, "blk", "cuts"),
        check_vma=False,
    )
```
